512 devices in a mesh: image: 16 (over x, y), space: 32 (over z, core).
Axes of the slice: x: 4, y: 4, z: 16, core: 2. Of those that a mesh axis runs over, the one named last changes fastest.
Arguments:
- positions: float32 [16, 3, 32768], P('image', None, 'space'), may hold values from -20 to 20
- neighbours: int32 [256, 3], replicated, may hold values from 0 to 4
- brackets: int32 [16], P('image'), may hold values from 0 to 14, as said below
- codes: int32 [16], P('image'), may hold values from 0 to 65535
Outputs:
- new_images: float32 [16, 3, 32768], P('image', None, 'space')
- arc_fraction: float32 [16], P('image')
The draws below stay inside these ranges and needn't reach their ends.
Inputs may be any that keep to these rules, and one draw needn't show every extreme that they name: brackets[j] lies between j - 1 and j + 1 - 1; both ends of that window are reached.
All inputs are finite; a program needn't handle non-finite values.
Results may differ from the reference program's by a relative error of at most 0.0003.
Values sent between devices are 32-bit elements; how exact they have to be, the bound alone decides.
A program may use at most 64 MiB of HBM per device.

```python
import jax
import jax.numpy as jnp
from jax import lax

IMG_DEV = 1
BEADS_DEV = 1024
PROT_DEV = 128
BLOCK = 128
HALO = 2
NEIGHBOURS = 3
STEPS = 10
IMAGES = 16
BEADS = 32768
NB = 8
BLOCKS = 256
N_SPACE = 32


def draw_positions(key, part):
    slabs = BEADS // BEADS_DEV
    first, second, third = jax.random.split(jax.random.fold_in(key, 11), 3)
    scales = jnp.exp(jax.random.uniform(first, (IMAGES, 1, slabs, 1), jnp.float32, 0.0, 1.39))
    noise = jnp.clip(jax.random.normal(second, (IMAGES, 3, slabs, BEADS_DEV), jnp.float32), -6.0, 6.0)
    common = 0.5 * jnp.clip(jax.random.normal(third, (1, 3, slabs, BEADS_DEV), jnp.float32), -6.0, 6.0)
    values = common + 0.5 * scales * noise
    return jnp.clip(values, -20.0, 20.0).reshape(IMAGES, 3, BEADS).astype(jnp.float32)


def draw_brackets(key, part):
    shifts = jax.random.randint(jax.random.fold_in(key, 5), (IMAGES,), -IMG_DEV, IMG_DEV, jnp.int32)
    shifts = shifts.at[IMG_DEV].set(-IMG_DEV)
    shifts = shifts.at[IMAGES - 2 * IMG_DEV].set(IMG_DEV - 1)
    centre = jnp.arange(IMAGES, dtype=jnp.int32)
    return jnp.clip(centre + shifts, 0, IMAGES - 2).astype(jnp.int32)


def with_ends(entries, key, least, high):
    shape = entries.shape
    spot = [jax.random.randint(jax.random.fold_in(key, axis), (), 0, shape[axis]) for axis in range(len(shape))]
    entries = entries.at[tuple(spot)].set(least)
    longest = shape.index(max(shape))
    spot[longest] = (spot[longest] + 1) % shape[longest]
    return entries.at[tuple(spot)].set(high)


def setup_inputs(seed: int = 0) -> dict:
    key_of = jax.random.split(jax.random.key(seed), 5)
    positions = draw_positions(jax.random.fold_in(key_of[4], 71), 0)
    neighbours = with_ends(jax.random.randint(key_of[1], (BLOCKS, NEIGHBOURS), 0, 2 * HALO + 1), jax.random.fold_in(key_of[1], 1), 0, 2 * HALO).astype(jnp.int32)
    brackets = draw_brackets(jax.random.fold_in(key_of[4], 71), 0)
    codes = with_ends(jax.random.randint(key_of[3], (IMAGES,), 0, 65536), jax.random.fold_in(key_of[3], 1), 0, 65535).astype(jnp.int32)
    return {"positions": positions, "neighbours": neighbours, "brackets": brackets, "codes": codes}


TIME_STEP = 0.05
RESTRAINT = 1.0
COUPLING = 3.0
KERNEL_RATE = 0.125
EPSILON = 1e-06
CODE_SCALE = 65536.0

def pair_forces(swarm_centres, partner_beads):
    centre_sq = lax.optimization_barrier(jnp.sum(swarm_centres * swarm_centres, axis=-3))
    partner_sq = lax.optimization_barrier(jnp.sum(partner_beads * partner_beads, axis=-3))
    crossing_flags = jnp.einsum('...euh,...euw->...uhw', swarm_centres, partner_beads, precision=lax.Precision.HIGHEST)
    weight_factors = jnp.exp(-KERNEL_RATE * (centre_sq[..., :, None] + partner_sq[..., None, :] - 2.0 * crossing_flags))
    row_sums = lax.optimization_barrier(jnp.sum(weight_factors, axis=-1))
    pulled_images = jnp.einsum('...aun,...san->...sau', weight_factors, partner_beads, precision=lax.Precision.HIGHEST)
    return COUPLING / partner_beads.shape[-1] * (swarm_centres * row_sums[..., None, :, :] - pulled_images)

def reference(positions, neighbours, brackets, codes):
    current = positions.reshape(IMAGES, 3, N_SPACE, NB, BLOCK)
    anchor = current
    bead_index = jnp.arange(NB * BLOCK, dtype=jnp.int32).reshape(NB, BLOCK)
    restrain = (bead_index < PROT_DEV).astype(jnp.float32)
    offset_table = neighbours.reshape(N_SPACE, NB, NEIGHBOURS)
    partner_blocks = (jnp.arange(NB, dtype=jnp.int32)[None, :, None] + offset_table).astype(jnp.int32)
    slab_ids = jnp.arange(N_SPACE, dtype=jnp.int32)[:, None, None]
    for turn_index in range(STEPS):
        left_rim = jnp.roll(current, 1, axis=2)[:, :, :, NB - HALO:]
        right_rim = jnp.roll(current, -1, axis=2)[:, :, :, :HALO]
        extended = jnp.concatenate([left_rim, current, right_rim], axis=3)

        def per_image(operands):
            image_ext, image_own = operands
            partner_beads = image_ext[:, slab_ids, partner_blocks]
            partner_beads = partner_beads.reshape(3, N_SPACE * NB, NEIGHBOURS * BLOCK)
            swarm_centres = image_own.reshape(3, N_SPACE * NB, BLOCK)
            return pair_forces(swarm_centres, partner_beads).reshape(3, N_SPACE, NB, BLOCK)
        forces = lax.map(per_image, (extended, current))
        current = current + TIME_STEP * (forces - RESTRAINT * restrain * (current - anchor))
    evolved = current.reshape(IMAGES, 3, N_SPACE * NB * BLOCK)
    protein = current.reshape(IMAGES, 3, N_SPACE, NB * BLOCK)[..., :PROT_DEV]
    differences = protein[1:] - protein[:-1]
    squares = lax.optimization_barrier(jnp.sum(differences * differences, axis=(1, 2, 3)))
    step_length = jnp.concatenate([jnp.zeros((1,), jnp.float32), jnp.sqrt(squares + EPSILON)])
    arc = jnp.cumsum(step_length)
    length_total = arc[IMAGES - 1]
    arc_fraction = arc / length_total
    target = (brackets.astype(jnp.float32) + codes.astype(jnp.float32) / CODE_SCALE) / (IMAGES - 1)
    arc_lower = arc[brackets]
    upper_arc_bound = arc[brackets + 1]
    weight = (target * length_total - arc_lower) / (upper_arc_bound - arc_lower)
    images_below = evolved[brackets]
    upper_images = evolved[brackets + 1]
    new_images = (1.0 - weight)[:, None, None] * images_below + weight[:, None, None] * upper_images
    return (new_images, arc_fraction)
```

```python
import functools
import math

import jax
import jax.numpy as jnp
from jax import lax
from jax.experimental import pallas as pl
from jax.experimental.pallas import tpu as pltpu
from jax.sharding import PartitionSpec as P

MESH = pl.DeviceIdType.MESH
F32, BF16 = jnp.float32, jnp.bfloat16

BLOCK = 128
HALO = 2
NB = 8
NEIGHBOURS = 3
IMAGES = 16
N_SPACE = 32
BLOCKS = NB * N_SPACE
TIME_STEP = 0.05
RESTRAINT = 1.0
COUPLING = 3.0
KERNEL_RATE = 0.125
EPSILON = 1e-06
CODE_SCALE = 65536.0

ROUNDS = (4, 3, 3)
OWN = NB
EXT = 3 * NB

SCALE = math.sqrt(KERNEL_RATE * math.log2(math.e))
PULL = TIME_STEP * COUPLING / (NEIGHBOURS * BLOCK)
PARTS = 32


def dot(a, b):
    return lax.dot_general(a, b, (((1,), (0,)), ((), ())), preferred_element_type=F32)


def split3(v):
    high = v.astype(BF16).astype(F32)
    rest = v - high
    middle = rest.astype(BF16).astype(F32)
    return high, middle, rest - middle


def operands(y):
    row = lax.broadcasted_iota(jnp.int32, y.shape, 1)
    y = jnp.where(row < 3, y, 0.0)
    square = jnp.sum(y * y, axis=1, keepdims=True)
    partner = jnp.where(row == 3, square, jnp.where(row == 4, 1.0, y))
    centre = jnp.where(row == 3, -1.0, jnp.where(row == 4, -square, y + y))
    ph, pm, plow = split3(partner)
    ch, cm, cl = split3(centre)
    a = jnp.concatenate([ph, ph, ph, pm, pm, plow], axis=1)
    b = jnp.concatenate([ch, cm, cl, ch, cm, ch], axis=1).astype(BF16)
    x = jnp.concatenate([ph, pm, plow, jnp.zeros_like(y)], axis=1).astype(BF16)
    return a, b, x


def kernel(x_ref, table, bracket, code, out_ref, fraction_ref, cur, anchor, aop, bop, xop, raw, got, around, plane, mine, part, parts, sems):
    image, slab = lax.axis_index("image"), lax.axis_index("space")

    def beside(d):
        return (image, lax.rem(slab + d + N_SPACE, N_SPACE))

    def across(d):
        return (lax.rem(image + d + IMAGES, IMAGES), slab)

    barrier = pltpu.get_barrier_semaphore()

    def greet_beside(d, _):
        pl.semaphore_signal(barrier, inc=1, device_id=beside(d), device_id_type=MESH)
        return 0

    def greet_across(d, _):
        pl.semaphore_signal(barrier, inc=1, device_id=across(d), device_id_type=MESH)
        return 0

    lax.fori_loop(1, N_SPACE, greet_beside, 0)
    lax.fori_loop(1, IMAGES, greet_across, 0)

    def store_operands(lo, y):
        a, b, x = operands(y)
        n = y.shape[0]
        bop[lo : lo + n] = b
        xop[lo : lo + n] = x
        for i in range(n):
            aop[lo + i] = a[i].T.astype(BF16)

    def take_slab(lo, slab_ref, scale):
        pad = jnp.zeros((NB, 5, BLOCK), F32)
        rows = [slab_ref[c].reshape(NB, 1, BLOCK) for c in range(3)]
        y = jnp.concatenate(rows + [pad], axis=1) * scale
        cur[lo : lo + NB] = y
        store_operands(lo, y)
        return y

    def exchange(r, source):
        copies = []
        for side, d in enumerate((1, -1)):
            copies.append(
                pltpu.make_async_remote_copy(
                    src_ref=source,
                    dst_ref=got.at[r, side],
                    send_sem=sems.at[0, 2 * r + side],
                    recv_sem=sems.at[1, 2 * r + side],
                    device_id=beside(d),
                    device_id_type=MESH,
                )
            )
        return copies

    own = take_slab(OWN, x_ref, SCALE)
    anchor[1] = own[0]
    pl.semaphore_wait(barrier, N_SPACE - 1 + IMAGES - 1)

    def step(lo, n):
        blocks = range(lo, lo + n)
        first = slab * NB + BLOCKS - OWN
        partners = [
            [e - HALO + table[k, lax.rem(first + e, BLOCKS)] for k in range(NEIGHBOURS)]
            for e in blocks
        ]
        weights = []
        for e, ps in zip(blocks, partners):
            exponent = dot(jnp.concatenate([aop[p] for p in ps], axis=0), bop[e])
            w = jnp.exp2(exponent)
            high = w.astype(BF16)
            weights.append(jnp.concatenate([high, (w - high.astype(F32)).astype(BF16)], axis=0))
        sums = []
        for ps, w in zip(partners, weights):
            x = jnp.concatenate([xop[p] for p in ps], axis=1)
            total = dot(jnp.concatenate([x, x], axis=1), w)
            sums.append(total[0:8] + total[8:16] + total[16:24])
        y = cur[lo : lo + n]
        total = jnp.stack(sums, axis=0)
        y_new = y + PULL * (y * total[:, 4:5] - total)
        held = [
            y_new[i : i + 1] - (TIME_STEP * RESTRAINT) * (y[i : i + 1] - anchor[e // NB][None])
            if e % NB == 0
            else y_new[i : i + 1]
            for i, e in enumerate(blocks)
        ]
        y_new = jnp.concatenate(held, axis=0)
        cur[lo : lo + n] = y_new
        return y_new

    def steps(count):
        for t in range(count):
            reach = HALO * (count - 1 - t)
            lo, n = OWN - reach, NB + 2 * reach
            y = step(lo, n)
            if t < count - 1:
                store_operands(lo, y)
        return y

    def pack(ref, y):
        for c in range(3):
            ref[c] = y[:, c]

    copies = exchange(0, x_ref)
    for c in copies:
        c.start()
    for c in copies:
        c.wait()
    anchor[0] = take_slab(0, got.at[0, 0], SCALE)[0]
    anchor[2] = take_slab(2 * NB, got.at[0, 1], SCALE)[0]
    y = steps(ROUNDS[0])
    for r in range(1, len(ROUNDS)):
        pack(raw.at[r], y)
        copies = exchange(r, raw.at[r])
        for c in copies:
            c.start()
        store_operands(OWN, y)
        for c in copies:
            c.wait()
        take_slab(0, got.at[r, 0], 1.0)
        take_slab(2 * NB, got.at[r, 1], 1.0)
        y = steps(ROUNDS[r])

    row = lax.broadcasted_iota(jnp.int32, (8, BLOCK), 0)
    mine[...] = jnp.where(row < 3, y[0], 0.0)[0:4]

    def send_protein(d, _):
        pltpu.make_async_remote_copy(
            src_ref=mine, dst_ref=plane.at[image], send_sem=sems.at[0, 6], recv_sem=sems.at[1, 6],
            device_id=across(d), device_id_type=MESH,
        ).start()
        return 0

    lax.fori_loop(1, IMAGES, send_protein, 0)
    pack(raw.at[0], y)
    images = [
        pltpu.make_async_remote_copy(
            src_ref=raw.at[0], dst_ref=around.at[side], send_sem=sems.at[0, 7 + side], recv_sem=sems.at[1, 7 + side],
            device_id=across(d), device_id_type=MESH,
        )
        for side, d in enumerate((1, -1))
    ]
    for c in images:
        c.start()
    others = plane.at[pl.ds(1, IMAGES - 1)]
    pltpu.make_async_copy(others, others, sems.at[1, 6]).wait()
    plane[image] = mine[...]

    every = plane[...]
    change = every[1:] - every[:-1]
    change = jnp.concatenate([jnp.zeros((1, 4, BLOCK), F32), change], axis=0)
    squares = jnp.sum(jnp.sum(change * change, axis=1), axis=1, keepdims=True)
    at_row = lax.broadcasted_iota(jnp.int32, (IMAGES, BLOCK), 0)
    at_lane = lax.broadcasted_iota(jnp.int32, (IMAGES, BLOCK), 1)
    part[...] = jnp.sum(jnp.where(at_row == at_lane, squares, 0.0), axis=0, keepdims=True)

    def send_part(d, _):
        pltpu.make_async_remote_copy(
            src_ref=part, dst_ref=parts.at[slab], send_sem=sems.at[0, 9], recv_sem=sems.at[1, 9],
            device_id=beside(d), device_id_type=MESH,
        ).start()
        return 0

    lax.fori_loop(1, N_SPACE, send_part, 0)
    for c in images:
        c.wait()
    pltpu.make_async_copy(others, others, sems.at[0, 6]).wait()
    rest = parts.at[pl.ds(1, N_SPACE - 1)]
    pltpu.make_async_copy(rest, rest, sems.at[1, 9]).wait()
    parts[slab] = part[...]

    lane = lax.broadcasted_iota(jnp.int32, (1, BLOCK), 1)
    total = jnp.sum(parts[...], axis=0)
    lengths = jnp.sqrt(total * (1.0 / SCALE**2) + EPSILON)
    lengths = jnp.where((lane > 0) & (lane < IMAGES), lengths, 0.0)

    def arc(k):
        return jnp.sum(jnp.where(lane <= k, lengths, 0.0), axis=1, keepdims=True)

    lower = bracket[0]
    full = arc(IMAGES - 1)
    arc_lower = arc(lower)
    place = jnp.full((1, 1), lower, jnp.int32).astype(F32) + jnp.full((1, 1), code[0], jnp.int32).astype(F32) / CODE_SCALE
    weight = (place / (IMAGES - 1) * full - arc_lower) / (arc(lower + 1) - arc_lower)
    fraction_ref[...] = jnp.broadcast_to(arc(image) / full, (1, BLOCK))
    earlier = lower < image
    for c in range(3):
        here = raw[0, c]
        below = jnp.where(earlier, around[0, c], here)
        above = jnp.where(earlier, here, around[1, c])
        out_ref[c] = ((1.0 - weight) * below + weight * above) * (1.0 / SCALE)
    pltpu.make_async_copy(rest, rest, sems.at[0, 9]).wait()


def body(positions, neighbours, brackets, codes):
    vmem, smem = (pl.BlockSpec(memory_space=s) for s in (pltpu.VMEM, pltpu.SMEM))
    rounds = len(ROUNDS)
    out, fraction = pl.pallas_call(
        kernel,
        out_shape=(jax.ShapeDtypeStruct((3, NB, BLOCK), F32), jax.ShapeDtypeStruct((1, BLOCK), F32)),
        in_specs=[vmem, smem, smem, smem],
        out_specs=(vmem, vmem),
        scratch_shapes=[
            pltpu.VMEM((EXT, 8, BLOCK), F32),
            pltpu.VMEM((3, 8, BLOCK), F32),
            pltpu.VMEM((EXT, BLOCK, 48), BF16),
            pltpu.VMEM((EXT, 48, BLOCK), BF16),
            pltpu.VMEM((EXT, 32, BLOCK), BF16),
            pltpu.VMEM((rounds, 3, NB, BLOCK), F32),
            pltpu.VMEM((rounds, 2, 3, NB, BLOCK), F32),
            pltpu.VMEM((2, 3, NB, BLOCK), F32),
            pltpu.VMEM((IMAGES, 4, BLOCK), F32),
            pltpu.VMEM((4, BLOCK), F32),
            pltpu.VMEM((1, BLOCK), F32),
            pltpu.VMEM((N_SPACE, 1, BLOCK), F32),
            pltpu.SemaphoreType.DMA((2, 10)),
        ],
        compiler_params=pltpu.CompilerParams(collective_id=0, has_side_effects=True, vmem_limit_bytes=48 << 20),
    )(positions.reshape(3, NB, BLOCK), neighbours.T, brackets, codes)
    return out.reshape(1, 3, NB * BLOCK), fraction[0, :1]


def solution(mesh):
    placed = (P("image", None, "space"), P(), P("image"), P("image"))
    return jax.shard_map(
        body,
        mesh=mesh,
        in_specs=placed,
        out_specs=(P("image", None, "space"), P("image")),
        check_vma=False,
    )
```

```python
import functools
import math

import jax
import jax.numpy as jnp
from jax import lax
from jax.experimental import pallas as pl
from jax.experimental.pallas import tpu as pltpu
from jax.sharding import PartitionSpec as P

MESH = pl.DeviceIdType.MESH
F32, BF16 = jnp.float32, jnp.bfloat16

BLOCK = 128
HALO = 2
NB = 8
NEIGHBOURS = 3
IMAGES = 16
N_SPACE = 32
BLOCKS = NB * N_SPACE
TIME_STEP = 0.05
RESTRAINT = 1.0
COUPLING = 3.0
KERNEL_RATE = 0.125
EPSILON = 1e-06
CODE_SCALE = 65536.0

ROUNDS = (4, 3, 3)
OWN = NB
EXT = 3 * NB

SCALE = math.sqrt(KERNEL_RATE * math.log2(math.e))
PULL = TIME_STEP * COUPLING / (NEIGHBOURS * BLOCK)
PARTS = 32


def dot(a, b):
    return lax.dot_general(a, b, (((1,), (0,)), ((), ())), preferred_element_type=F32)


def split3(v):
    high = v.astype(BF16).astype(F32)
    rest = v - high
    middle = rest.astype(BF16).astype(F32)
    return high, middle, rest - middle


def operands(y):
    row = lax.broadcasted_iota(jnp.int32, y.shape, 1)
    y = jnp.where(row < 3, y, 0.0)
    square = jnp.sum(y * y, axis=1, keepdims=True)
    partner = jnp.where(row == 3, square, jnp.where(row == 4, 1.0, y))
    centre = jnp.where(row == 3, -1.0, jnp.where(row == 4, -square, y + y))
    ph, pm, plow = split3(partner)
    ch, cm, cl = split3(centre)
    a = jnp.concatenate([ph, ph, ph, pm, pm, plow], axis=1)
    b = jnp.concatenate([ch, cm, cl, ch, cm, ch], axis=1).astype(BF16)
    x = jnp.concatenate([ph, pm, plow, jnp.zeros_like(y)], axis=1).astype(BF16)
    return a, b, x


def kernel(
    x_ref, table_in, images_ref, total_ref,
    table, local_sem, relay_sems, cur, anchor, aop, bop, xop, raw, got, around, plane, mine, part, parts, sems,
):
    image, slab = lax.axis_index("image"), lax.axis_index("space")

    def beside(d):
        return (image, lax.rem(slab + d + N_SPACE, N_SPACE))

    def across(d):
        return (lax.rem(image + d + IMAGES, IMAGES), slab)

    ring = sorted(range(1, N_SPACE), key=lambda d: -min(d, N_SPACE - d))
    square = [(dx, dy) for dx in range(4) for dy in range(4) if (dx, dy) != (0, 0)]
    square.sort(key=lambda d: -sum(min(v, 4 - v) for v in d))

    def in_plane(d):
        return (lax.rem(image // 4 + d[0], 4) * 4 + lax.rem(lax.rem(image, 4) + d[1], 4), slab)

    def greet(semaphore, peers):
        for peer in peers:
            pl.semaphore_signal(semaphore, inc=1, device_id=peer, device_id_type=MESH)

    barrier = pltpu.get_barrier_semaphore()
    near = [beside(1), beside(-1), across(1), across(-1)]
    stages = [
        [peer for far in reach for peer in far]
        for reach in (
            [(beside(1), beside(-1)), (across(1), across(-1))],
            [(beside(2), beside(-2)), (across(2), across(-2))],
            [(beside(4), beside(-4)), (across(4), across(-4))],
            [(beside(8), beside(-8))],
        )
    ]

    def relay(j):
        if j > 0:
            pl.semaphore_wait(relay_sems.at[j - 1], len(stages[j - 1]))
        if j < len(stages):
            greet(relay_sems.at[j], stages[j])

    greet(barrier, near)
    load = pltpu.make_async_copy(table_in, table, local_sem)
    load.start()

    def store_operands(lo, y):
        a, b, x = operands(y)
        n = y.shape[0]
        bop[lo : lo + n] = b
        xop[lo : lo + n] = x
        for i in range(n):
            aop[lo + i] = a[i].T.astype(BF16)

    def take_slab(lo, slab_ref, scale):
        pad = jnp.zeros((NB, 5, BLOCK), F32)
        rows = [slab_ref[c].reshape(NB, 1, BLOCK) for c in range(3)]
        y = jnp.concatenate(rows + [pad], axis=1) * scale
        cur[lo : lo + NB] = y
        store_operands(lo, y)
        return y

    def exchange(r, source):
        copies = []
        for side, d in enumerate((1, -1)):
            copies.append(
                pltpu.make_async_remote_copy(
                    src_ref=source,
                    dst_ref=got.at[r, side],
                    send_sem=sems.at[0, 2 * r + side],
                    recv_sem=sems.at[1, 2 * r + side],
                    device_id=beside(d),
                    device_id_type=MESH,
                )
            )
        return copies

    pl.semaphore_wait(barrier, len(near))
    copies = exchange(0, x_ref)
    for c in copies:
        c.start()
    relay(0)
    own = take_slab(OWN, x_ref, SCALE)
    anchor[1] = own[0]
    load.wait()

    def step(lo, n):
        blocks = range(lo, lo + n)
        first = slab * NB + BLOCKS - OWN
        partners = [
            [e - HALO + table[k, lax.rem(first + e, BLOCKS)] for k in range(NEIGHBOURS)]
            for e in blocks
        ]
        weights = []
        for e, ps in zip(blocks, partners):
            exponent = dot(jnp.concatenate([aop[p] for p in ps], axis=0), bop[e])
            w = jnp.exp2(exponent)
            high = w.astype(BF16)
            weights.append(jnp.concatenate([high, (w - high.astype(F32)).astype(BF16)], axis=0))
        sums = []
        for ps, w in zip(partners, weights):
            x = jnp.concatenate([xop[p] for p in ps], axis=1)
            total = dot(jnp.concatenate([x, x], axis=1), w)
            sums.append(total[0:8] + total[8:16] + total[16:24])
        y = cur[lo : lo + n]
        total = jnp.stack(sums, axis=0)
        y_new = y + PULL * (y * total[:, 4:5] - total)
        held = [
            y_new[i : i + 1] - (TIME_STEP * RESTRAINT) * (y[i : i + 1] - anchor[e // NB][None])
            if e % NB == 0
            else y_new[i : i + 1]
            for i, e in enumerate(blocks)
        ]
        y_new = jnp.concatenate(held, axis=0)
        cur[lo : lo + n] = y_new
        return y_new

    def steps(count, last, between):
        for t in range(count - last):
            reach = HALO * (count - 1 - t)
            lo, n = OWN - reach, NB + 2 * reach
            y = step(lo, n)
            if t < count - 1:
                store_operands(lo, y)
            if t in between:
                relay(between[t])
        return y

    def pack(ref, y):
        for c in range(3):
            ref[c] = y[:, c]

    for c in copies:
        c.wait()
    relay(1)
    anchor[0] = take_slab(0, got.at[0, 0], SCALE)[0]
    anchor[2] = take_slab(2 * NB, got.at[0, 1], SCALE)[0]
    y = steps(ROUNDS[0], 0, {1: 2})
    for r in range(1, len(ROUNDS)):
        pack(raw.at[r], y)
        copies = exchange(r, raw.at[r])
        for c in copies:
            c.start()
        store_operands(OWN, y)
        for c in copies:
            c.wait()
        take_slab(0, got.at[r, 0], 1.0)
        take_slab(2 * NB, got.at[r, 1], 1.0)
        if r == 1:
            relay(3)
        y = steps(ROUNDS[r], int(r == len(ROUNDS) - 1), {})
    relay(4)

    row = lax.broadcasted_iota(jnp.int32, (8, BLOCK), 0)
    head = step(OWN, 1)
    mine[...] = jnp.where(row < 3, head[0], 0.0)[0:4]
    for d in square:
        pltpu.make_async_remote_copy(
            src_ref=mine, dst_ref=plane.at[image], send_sem=sems.at[0, 6], recv_sem=sems.at[1, 6],
            device_id=in_plane(d), device_id_type=MESH,
        ).start()
    pack(raw.at[0], jnp.concatenate([head, step(OWN + 1, NB - 1)], axis=0))
    images = [
        pltpu.make_async_remote_copy(
            src_ref=raw.at[0], dst_ref=around.at[side], send_sem=sems.at[0, 7 + side], recv_sem=sems.at[1, 7 + side],
            device_id=across(d), device_id_type=MESH,
        )
        for side, d in enumerate((1, -1))
    ]
    for c in images:
        c.start()
    others = plane.at[pl.ds(1, IMAGES - 1)]
    pltpu.make_async_copy(others, others, sems.at[1, 6]).wait()
    plane[image] = mine[...]

    every = plane[...]
    change = every[1:] - every[:-1]
    change = jnp.concatenate([jnp.zeros((1, 4, BLOCK), F32), change], axis=0)
    squares = jnp.sum(jnp.sum(change * change, axis=1), axis=1, keepdims=True)
    at_row = lax.broadcasted_iota(jnp.int32, (IMAGES, BLOCK), 0)
    at_lane = lax.broadcasted_iota(jnp.int32, (IMAGES, BLOCK), 1)
    part[...] = jnp.sum(jnp.where(at_row == at_lane, squares, 0.0), axis=0, keepdims=True)

    for d in ring:
        pltpu.make_async_remote_copy(
            src_ref=part, dst_ref=parts.at[slab], send_sem=sems.at[0, 9], recv_sem=sems.at[1, 9],
            device_id=beside(d), device_id_type=MESH,
        ).start()
    for c in images:
        c.wait()
    pltpu.make_async_copy(others, others, sems.at[0, 6]).wait()
    rest = parts.at[pl.ds(1, N_SPACE - 1)]
    pltpu.make_async_copy(rest, rest, sems.at[1, 9]).wait()
    parts[slab] = part[...]

    total_ref[...] = jnp.sum(parts[...], axis=0)
    images_ref[0] = around[0]
    images_ref[1] = raw[0]
    images_ref[2] = around[1]
    pltpu.make_async_copy(rest, rest, sems.at[0, 9]).wait()


def blend(images_ref, total_ref, whole_ref, out_ref, fraction_ref, out, fraction, sems):
    image = lax.axis_index("image")
    lane = lax.broadcasted_iota(jnp.int32, (1, BLOCK), 1)
    lengths = jnp.sqrt(total_ref[...] * (1.0 / SCALE**2) + EPSILON)
    lengths = jnp.where((lane > 0) & (lane < IMAGES), lengths, 0.0)

    def arc(k):
        return jnp.sum(jnp.where(lane <= k, lengths, 0.0), axis=1, keepdims=True)

    full = arc(IMAGES - 1)
    fraction[...] = jnp.broadcast_to(arc(image) / full, (1, BLOCK))
    lower = whole_ref[NEIGHBOURS : NEIGHBOURS + 1, :BLOCK]
    code = whole_ref[NEIGHBOURS + 1 : NEIGHBOURS + 2, :BLOCK]
    arc_lower = arc(lower)
    place = lower.astype(F32) + code.astype(F32) / CODE_SCALE
    weight = (place / (IMAGES - 1) * full - arc_lower) / (arc(lower + 1) - arc_lower)
    earlier = lower < image
    for c in range(3):
        here = images_ref[1, c]
        below = jnp.where(earlier, images_ref[0, c], here)
        above = jnp.where(earlier, here, images_ref[2, c])
        out[c] = ((1.0 - weight) * below + weight * above) * (1.0 / SCALE)
    stores = [pltpu.make_async_copy(s, d, sems.at[i]) for i, (s, d) in enumerate([(out, out_ref), (fraction, fraction_ref)])]
    for c in stores:
        c.start()
    for c in stores:
        c.wait()


def body(positions, neighbours, brackets, codes):
    vmem = pl.BlockSpec(memory_space=pltpu.VMEM)
    rounds = len(ROUNDS)
    along = [jnp.broadcast_to(v[:, None], (1, BLOCKS)) for v in (brackets, codes)]
    whole = jnp.concatenate([neighbours.T] + along, axis=0)
    images, total = pl.pallas_call(
        kernel,
        out_shape=(jax.ShapeDtypeStruct((3, 3, NB, BLOCK), F32), jax.ShapeDtypeStruct((1, BLOCK), F32)),
        in_specs=[vmem] * 2,
        out_specs=(vmem, vmem),
        scratch_shapes=[
            pltpu.SMEM((NEIGHBOURS + 2, BLOCKS), jnp.int32),
            pltpu.SemaphoreType.DMA,
            pltpu.SemaphoreType.REGULAR((4,)),
            pltpu.VMEM((EXT, 8, BLOCK), F32),
            pltpu.VMEM((3, 8, BLOCK), F32),
            pltpu.VMEM((EXT, BLOCK, 48), BF16),
            pltpu.VMEM((EXT, 48, BLOCK), BF16),
            pltpu.VMEM((EXT, 32, BLOCK), BF16),
            pltpu.VMEM((rounds, 3, NB, BLOCK), F32),
            pltpu.VMEM((rounds, 2, 3, NB, BLOCK), F32),
            pltpu.VMEM((2, 3, NB, BLOCK), F32),
            pltpu.VMEM((IMAGES, 4, BLOCK), F32),
            pltpu.VMEM((4, BLOCK), F32),
            pltpu.VMEM((1, BLOCK), F32),
            pltpu.VMEM((N_SPACE, 1, BLOCK), F32),
            pltpu.SemaphoreType.DMA((2, 10)),
        ],
        compiler_params=pltpu.CompilerParams(collective_id=0, has_side_effects=True, vmem_limit_bytes=48 << 20),
    )(positions.reshape(3, NB, BLOCK), whole)
    hbm = pl.BlockSpec(memory_space=pl.ANY)
    out, fraction = pl.pallas_call(
        blend,
        out_shape=(jax.ShapeDtypeStruct((3, NB, BLOCK), F32), jax.ShapeDtypeStruct((1, BLOCK), F32)),
        in_specs=[vmem] * 3,
        out_specs=(hbm, hbm),
        scratch_shapes=[
            pltpu.VMEM((3, NB, BLOCK), F32),
            pltpu.VMEM((1, BLOCK), F32),
            pltpu.SemaphoreType.DMA((2,)),
        ],
        compiler_params=pltpu.CompilerParams(vmem_limit_bytes=16 << 20),
    )(images, total, whole)
    return out.reshape(1, 3, NB * BLOCK), fraction[0, :1]


def solution(mesh):
    placed = (P("image", None, "space"), P(), P("image"), P("image"))
    return jax.shard_map(
        body,
        mesh=mesh,
        in_specs=placed,
        out_specs=(P("image", None, "space"), P("image")),
        check_vma=False,
    )
```

```python
import functools
import math

import jax
import jax.numpy as jnp
from jax import lax
from jax.experimental import pallas as pl
from jax.experimental.pallas import tpu as pltpu
from jax.sharding import PartitionSpec as P

MESH = pl.DeviceIdType.MESH
F32, BF16 = jnp.float32, jnp.bfloat16

BLOCK = 128
HALO = 2
NB = 8
NEIGHBOURS = 3
IMAGES = 16
N_SPACE = 32
BLOCKS = NB * N_SPACE
TIME_STEP = 0.05
RESTRAINT = 1.0
COUPLING = 3.0
KERNEL_RATE = 0.125
EPSILON = 1e-06
CODE_SCALE = 65536.0

FIRST, LAST = 4, 6
OWN = 2 * NB
EXT = 5 * NB

SCALE = math.sqrt(KERNEL_RATE * math.log2(math.e))
PULL = TIME_STEP * COUPLING / (NEIGHBOURS * BLOCK)


def dot(a, b):
    return lax.dot_general(a, b, (((1,), (0,)), ((), ())), preferred_element_type=F32)


def split3(v):
    high = v.astype(BF16).astype(F32)
    rest = v - high
    middle = rest.astype(BF16).astype(F32)
    return high, middle, rest - middle


def operands(y):
    row = lax.broadcasted_iota(jnp.int32, y.shape, 1)
    y = jnp.where(row < 3, y, 0.0)
    square = jnp.sum(y * y, axis=1, keepdims=True)
    partner = jnp.where(row == 3, square, jnp.where(row == 4, 1.0, y))
    centre = jnp.where(row == 3, -1.0, jnp.where(row == 4, -square, y + y))
    ph, pm, plow = split3(partner)
    ch, cm, cl = split3(centre)
    a = jnp.concatenate([ph, ph, ph, pm, pm, plow], axis=1)
    b = jnp.concatenate([ch, cm, cl, ch, cm, ch], axis=1).astype(BF16)
    x = jnp.concatenate([ph, pm, plow, jnp.zeros_like(y)], axis=1).astype(BF16)
    return a, b, x


def kernel(
    x_ref, table_in, images_ref, total_ref,
    table, local_sem, relay_sems, cur, anchor, aop, bop, xop, raw, got, around, plane, mine, part, parts, sems,
):
    image, slab = lax.axis_index("image"), lax.axis_index("space")

    def beside(d):
        return (image, lax.rem(slab + d + N_SPACE, N_SPACE))

    def across(d):
        return (lax.rem(image + d + IMAGES, IMAGES), slab)

    ring = sorted(range(1, N_SPACE), key=lambda d: -min(d, N_SPACE - d))
    square = [(dx, dy) for dx in range(4) for dy in range(4) if (dx, dy) != (0, 0)]
    square.sort(key=lambda d: -sum(min(v, 4 - v) for v in d))

    def in_plane(d):
        return (lax.rem(image // 4 + d[0], 4) * 4 + lax.rem(lax.rem(image, 4) + d[1], 4), slab)

    def greet(semaphore, peers):
        for peer in peers:
            pl.semaphore_signal(semaphore, inc=1, device_id=peer, device_id_type=MESH)

    barrier = pltpu.get_barrier_semaphore()
    near = [beside(1), beside(-1), across(1), across(-1)]
    stages = [
        [peer for far in reach for peer in far]
        for reach in (
            [(beside(1), beside(-1)), (across(1), across(-1))],
            [(beside(2), beside(-2)), (across(2), across(-2))],
            [(beside(4), beside(-4)), (across(4), across(-4))],
            [(beside(8), beside(-8))],
        )
    ]

    def relay(j):
        if j > 0:
            pl.semaphore_wait(relay_sems.at[j - 1], len(stages[j - 1]))
        if j < len(stages):
            greet(relay_sems.at[j], stages[j])

    greet(barrier, near)
    load = pltpu.make_async_copy(table_in, table, local_sem)
    load.start()

    def store(version, lo, y):
        a, b, x = operands(y)
        n = y.shape[0]
        cur[version, lo : lo + n] = y
        bop[version, lo : lo + n] = b
        xop[version, lo : lo + n] = x
        for i in range(n):
            aop[version, lo + i] = a[i].T.astype(BF16)

    def rows(slab_ref, first, last):
        n = last - first
        coordinates = [slab_ref[c, first:last].reshape(n, 1, BLOCK) for c in range(3)]
        return jnp.concatenate(coordinates + [jnp.zeros((n, 5, BLOCK), F32)], axis=1)

    def send(source, target, slot, peer):
        return pltpu.make_async_remote_copy(
            src_ref=source, dst_ref=target, send_sem=sems.at[0, slot], recv_sem=sems.at[1, slot],
            device_id=peer, device_id_type=MESH,
        )

    def step(version, lo, n):
        blocks = range(lo, lo + n)
        first = slab * NB + BLOCKS - OWN
        partners = [
            [e - HALO + table[k, lax.rem(first + e, BLOCKS)] for k in range(NEIGHBOURS)]
            for e in blocks
        ]
        weights = []
        for e, ps in zip(blocks, partners):
            exponent = dot(jnp.concatenate([aop[version, p] for p in ps], axis=0), bop[version, e])
            w = jnp.exp2(exponent)
            high = w.astype(BF16)
            weights.append(jnp.concatenate([high, (w - high.astype(F32)).astype(BF16)], axis=0))
        sums = []
        for ps, w in zip(partners, weights):
            x = jnp.concatenate([xop[version, p] for p in ps], axis=1)
            total = dot(jnp.concatenate([x, x], axis=1), w)
            sums.append(total[0:8] + total[8:16] + total[16:24])
        y = cur[version, lo : lo + n]
        total = jnp.stack(sums, axis=0)
        y_new = y + PULL * (y * total[:, 4:5] - total)
        held = [
            y_new[i : i + 1] - (TIME_STEP * RESTRAINT) * (y[i : i + 1] - anchor[e // NB][None])
            if e % NB == 0
            else y_new[i : i + 1]
            for i, e in enumerate(blocks)
        ]
        return jnp.concatenate(held, axis=0) if n > 1 else held[0]

    def pack(ref, y):
        for c in range(3):
            ref[c] = y[:, c]

    pl.semaphore_wait(barrier, len(near))
    from_left, from_right, from_right2 = (got.at[i] for i in range(3))
    beginning = [send(x_ref, from_left, 0, beside(1)), send(x_ref, from_right, 1, beside(-1))]
    for c in beginning:
        c.start()
    relay(0)
    own = rows(x_ref, 0, NB) * SCALE
    anchor[2] = own[0]
    store(0, OWN, own)
    load.wait()
    for c in beginning:
        c.wait()
    relay(1)
    later = send(x_ref, from_right2, 2, beside(-2))
    later.start()
    left = rows(from_left, 0, NB) * SCALE
    right = rows(from_right, 0, NB) * SCALE
    anchor[1] = left[0]
    anchor[3] = right[0]
    store(0, OWN - NB, left)
    store(0, OWN + NB, right)
    for t in range(FIRST):
        reach = HALO * (FIRST - 1 - t)
        y = step(0, OWN - reach, NB + 2 * reach)
        if t < FIRST - 1:
            store(0, OWN - reach, y)
        if t == 1:
            relay(2)

    pack(raw.at[1], y)
    middle = [send(raw.at[1], got.at[3 + i], 3 + i, beside(d)) for i, d in enumerate((2, -2, 1, -1))]
    for c in middle:
        c.start()
    store(0, OWN, y)
    for c in middle:
        c.wait()
    relay(3)
    left2, right2, left, right = (got.at[3 + i] for i in range(4))
    reach = HALO * LAST - NB
    store(0, OWN - NB - reach, jnp.concatenate([rows(left2, NB - reach, NB), rows(left, 0, NB)], axis=0))
    store(0, OWN + NB, rows(right, 0, reach + 1))

    for s in range(1, LAST + 1):
        reach = HALO * (LAST - s)
        head = step(s - 1, OWN - reach, 2 * reach + 1)
        if s < LAST:
            store(s, OWN - reach, head)
    relay(4)

    row = lax.broadcasted_iota(jnp.int32, (8, BLOCK), 0)
    mine[...] = jnp.where(row < 3, head[0], 0.0)[0:4]
    for d in square:
        send(mine, plane.at[image], 7, in_plane(d)).start()

    later.wait()
    anchor[4] = rows(from_right2, 0, 1)[0] * SCALE
    reach = HALO * LAST - NB
    store(0, OWN + NB + reach + 1, jnp.concatenate([rows(right, reach + 1, NB), rows(right2, 0, reach)], axis=0))

    def rest_of_step(s):
        lo = OWN + HALO * (LAST - s) + 1
        y = step(s - 1, lo, NB - 1)
        if s < LAST:
            store(s, lo, y)
        return y

    for s in range(1, LAST):
        rest_of_step(s)
    others = plane.at[pl.ds(1, IMAGES - 1)]
    pltpu.make_async_copy(others, others, sems.at[1, 7]).wait()
    plane[image] = mine[...]

    every = plane[...]
    change = every[1:] - every[:-1]
    change = jnp.concatenate([jnp.zeros((1, 4, BLOCK), F32), change], axis=0)
    squares = jnp.sum(jnp.sum(change * change, axis=1), axis=1, keepdims=True)
    at_row = lax.broadcasted_iota(jnp.int32, (IMAGES, BLOCK), 0)
    at_lane = lax.broadcasted_iota(jnp.int32, (IMAGES, BLOCK), 1)
    part[...] = jnp.sum(jnp.where(at_row == at_lane, squares, 0.0), axis=0, keepdims=True)

    for d in ring:
        send(part, parts.at[slab], 10, beside(d)).start()
    pack(raw.at[0], jnp.concatenate([head, rest_of_step(LAST)], axis=0))
    images = [send(raw.at[0], around.at[i], 8 + i, across(d)) for i, d in enumerate((1, -1))]
    for c in images:
        c.start()
    for c in images:
        c.wait()
    pltpu.make_async_copy(others, others, sems.at[0, 7]).wait()
    rest = parts.at[pl.ds(1, N_SPACE - 1)]
    pltpu.make_async_copy(rest, rest, sems.at[1, 10]).wait()
    parts[slab] = part[...]

    total_ref[...] = jnp.sum(parts[...], axis=0)
    images_ref[0] = around[0]
    images_ref[1] = raw[0]
    images_ref[2] = around[1]
    pltpu.make_async_copy(rest, rest, sems.at[0, 10]).wait()


def blend(images_ref, total_ref, whole_ref, out_ref, fraction_ref, out, fraction, sems):
    image = lax.axis_index("image")
    lane = lax.broadcasted_iota(jnp.int32, (1, BLOCK), 1)
    lengths = jnp.sqrt(total_ref[...] * (1.0 / SCALE**2) + EPSILON)
    lengths = jnp.where((lane > 0) & (lane < IMAGES), lengths, 0.0)

    def arc(k):
        return jnp.sum(jnp.where(lane <= k, lengths, 0.0), axis=1, keepdims=True)

    full = arc(IMAGES - 1)
    fraction[...] = jnp.broadcast_to(arc(image) / full, (1, BLOCK))
    lower = whole_ref[NEIGHBOURS : NEIGHBOURS + 1, :BLOCK]
    code = whole_ref[NEIGHBOURS + 1 : NEIGHBOURS + 2, :BLOCK]
    arc_lower = arc(lower)
    place = lower.astype(F32) + code.astype(F32) / CODE_SCALE
    weight = (place / (IMAGES - 1) * full - arc_lower) / (arc(lower + 1) - arc_lower)
    earlier = lower < image
    for c in range(3):
        here = images_ref[1, c]
        below = jnp.where(earlier, images_ref[0, c], here)
        above = jnp.where(earlier, here, images_ref[2, c])
        out[c] = ((1.0 - weight) * below + weight * above) * (1.0 / SCALE)
    stores = [pltpu.make_async_copy(s, d, sems.at[i]) for i, (s, d) in enumerate([(out, out_ref), (fraction, fraction_ref)])]
    for c in stores:
        c.start()
    for c in stores:
        c.wait()


def body(positions, neighbours, brackets, codes):
    vmem = pl.BlockSpec(memory_space=pltpu.VMEM)
    along = [jnp.broadcast_to(v[:, None], (1, BLOCKS)) for v in (brackets, codes)]
    whole = jnp.concatenate([neighbours.T] + along, axis=0)
    images, total = pl.pallas_call(
        kernel,
        out_shape=(jax.ShapeDtypeStruct((3, 3, NB, BLOCK), F32), jax.ShapeDtypeStruct((1, BLOCK), F32)),
        in_specs=[vmem] * 2,
        out_specs=(vmem, vmem),
        scratch_shapes=[
            pltpu.SMEM((NEIGHBOURS + 2, BLOCKS), jnp.int32),
            pltpu.SemaphoreType.DMA,
            pltpu.SemaphoreType.REGULAR((4,)),
            pltpu.VMEM((LAST, EXT, 8, BLOCK), F32),
            pltpu.VMEM((EXT // NB, 8, BLOCK), F32),
            pltpu.VMEM((LAST, EXT, BLOCK, 48), BF16),
            pltpu.VMEM((LAST, EXT, 48, BLOCK), BF16),
            pltpu.VMEM((LAST, EXT, 32, BLOCK), BF16),
            pltpu.VMEM((2, 3, NB, BLOCK), F32),
            pltpu.VMEM((7, 3, NB, BLOCK), F32),
            pltpu.VMEM((2, 3, NB, BLOCK), F32),
            pltpu.VMEM((IMAGES, 4, BLOCK), F32),
            pltpu.VMEM((4, BLOCK), F32),
            pltpu.VMEM((1, BLOCK), F32),
            pltpu.VMEM((N_SPACE, 1, BLOCK), F32),
            pltpu.SemaphoreType.DMA((2, 11)),
        ],
        compiler_params=pltpu.CompilerParams(collective_id=0, has_side_effects=True, vmem_limit_bytes=48 << 20),
    )(positions.reshape(3, NB, BLOCK), whole)
    hbm = pl.BlockSpec(memory_space=pl.ANY)
    out, fraction = pl.pallas_call(
        blend,
        out_shape=(jax.ShapeDtypeStruct((3, NB, BLOCK), F32), jax.ShapeDtypeStruct((1, BLOCK), F32)),
        in_specs=[vmem] * 3,
        out_specs=(hbm, hbm),
        scratch_shapes=[
            pltpu.VMEM((3, NB, BLOCK), F32),
            pltpu.VMEM((1, BLOCK), F32),
            pltpu.SemaphoreType.DMA((2,)),
        ],
        compiler_params=pltpu.CompilerParams(vmem_limit_bytes=16 << 20),
    )(images, total, whole)
    return out.reshape(1, 3, NB * BLOCK), fraction[0, :1]


def solution(mesh):
    placed = (P("image", None, "space"), P(), P("image"), P("image"))
    return jax.shard_map(
        body,
        mesh=mesh,
        in_specs=placed,
        out_specs=(P("image", None, "space"), P("image")),
        check_vma=False,
    )
```

```python
import functools
import math

import jax
import jax.numpy as jnp
from jax import lax
from jax.experimental import pallas as pl
from jax.experimental.pallas import tpu as pltpu
from jax.sharding import PartitionSpec as P

MESH = pl.DeviceIdType.MESH
F32, BF16 = jnp.float32, jnp.bfloat16

BLOCK = 128
HALO = 2
NB = 8
NEIGHBOURS = 3
IMAGES = 16
N_SPACE = 32
BLOCKS = NB * N_SPACE
TIME_STEP = 0.05
RESTRAINT = 1.0
COUPLING = 3.0
KERNEL_RATE = 0.125
EPSILON = 1e-06
CODE_SCALE = 65536.0

FIRST, LAST = 4, 6
OWN = 2 * NB
EXT = 5 * NB

SCALE = math.sqrt(KERNEL_RATE * math.log2(math.e))
PULL = TIME_STEP * COUPLING / (NEIGHBOURS * BLOCK)


def dot(a, b):
    return lax.dot_general(a, b, (((1,), (0,)), ((), ())), preferred_element_type=F32)


def split3(v):
    high = v.astype(BF16).astype(F32)
    rest = v - high
    middle = rest.astype(BF16).astype(F32)
    return high, middle, rest - middle


def operands(y):
    row = lax.broadcasted_iota(jnp.int32, y.shape, 1)
    y = jnp.where(row < 3, y, 0.0)
    square = jnp.sum(y * y, axis=1, keepdims=True)
    partner = jnp.where(row == 3, square, jnp.where(row == 4, 1.0, y))
    centre = jnp.where(row == 3, -1.0, jnp.where(row == 4, -square, y + y))
    ph, pm, plow = split3(partner)
    ch, cm, cl = split3(centre)
    a = jnp.concatenate([ph, ph, ph, pm, pm, plow], axis=1)
    b = jnp.concatenate([ch, cm, cl, ch, cm, ch], axis=1).astype(BF16)
    x = jnp.concatenate([ph, pm, plow, jnp.zeros_like(y)], axis=1).astype(BF16)
    return a, b, x


def kernel(
    x_ref, left_ref, right_ref, table_in, images_ref, total_ref,
    table, local_sem, relay_sems, cur, anchor, aop, bop, xop, raw, got, around, plane, mine, part, parts, sems,
):
    image, slab = lax.axis_index("image"), lax.axis_index("space")

    def beside(d):
        return (image, lax.rem(slab + d + N_SPACE, N_SPACE))

    def across(d):
        return (lax.rem(image + d + IMAGES, IMAGES), slab)

    ring = sorted(range(1, N_SPACE), key=lambda d: -min(d, N_SPACE - d))
    square = [(dx, dy) for dx in range(4) for dy in range(4) if (dx, dy) != (0, 0)]
    square.sort(key=lambda d: -sum(min(v, 4 - v) for v in d))

    def in_plane(d):
        return (lax.rem(image // 4 + d[0], 4) * 4 + lax.rem(lax.rem(image, 4) + d[1], 4), slab)

    def greet(semaphore, peers):
        for peer in peers:
            pl.semaphore_signal(semaphore, inc=1, device_id=peer, device_id_type=MESH)

    barrier = pltpu.get_barrier_semaphore()
    near = [peer for d in (1, -1, 2, -2) for peer in (beside(d), across(d))]
    stages = [
        [peer for d in (2, -2) for peer in (beside(d), across(d))],
        [peer for d in (4, -4) for peer in (beside(d), across(d))],
        [beside(8), beside(-8)],
    ]

    def relay(j):
        if j > 0:
            pl.semaphore_wait(relay_sems.at[j - 1], len(stages[j - 1]))
        if j < len(stages):
            greet(relay_sems.at[j], stages[j])

    greet(barrier, near)
    load = pltpu.make_async_copy(table_in, table, local_sem)
    load.start()

    def store(version, lo, y):
        a, b, x = operands(y)
        n = y.shape[0]
        cur[version, lo : lo + n] = y
        bop[version, lo : lo + n] = b
        xop[version, lo : lo + n] = x
        for i in range(n):
            aop[version, lo + i] = a[i].T.astype(BF16)

    def rows(slab_ref, first, last):
        n = last - first
        coordinates = [slab_ref[c, first:last].reshape(n, 1, BLOCK) for c in range(3)]
        return jnp.concatenate(coordinates + [jnp.zeros((n, 5, BLOCK), F32)], axis=1)

    def send(source, target, slot, peer):
        return pltpu.make_async_remote_copy(
            src_ref=source, dst_ref=target, send_sem=sems.at[0, slot], recv_sem=sems.at[1, slot],
            device_id=peer, device_id_type=MESH,
        )

    def step(version, lo, n):
        blocks = range(lo, lo + n)
        first = slab * NB + BLOCKS - OWN
        partners = [
            [e - HALO + table[k, lax.rem(first + e, BLOCKS)] for k in range(NEIGHBOURS)]
            for e in blocks
        ]
        weights = []
        for e, ps in zip(blocks, partners):
            exponent = dot(jnp.concatenate([aop[version, p] for p in ps], axis=0), bop[version, e])
            w = jnp.exp2(exponent)
            high = w.astype(BF16)
            weights.append(jnp.concatenate([high, (w - high.astype(F32)).astype(BF16)], axis=0))
        sums = []
        for ps, w in zip(partners, weights):
            x = jnp.concatenate([xop[version, p] for p in ps], axis=1)
            total = dot(jnp.concatenate([x, x], axis=1), w)
            sums.append(total[0:8] + total[8:16] + total[16:24])
        y = cur[version, lo : lo + n]
        total = jnp.stack(sums, axis=0)
        y_new = y + PULL * (y * total[:, 4:5] - total)
        held = [
            y_new[i : i + 1] - (TIME_STEP * RESTRAINT) * (y[i : i + 1] - anchor[e // NB][None])
            if e % NB == 0
            else y_new[i : i + 1]
            for i, e in enumerate(blocks)
        ]
        return jnp.concatenate(held, axis=0) if n > 1 else held[0]

    def pack(ref, y):
        for c in range(3):
            ref[c] = y[:, c]

    own, left, right = (rows(ref, 0, NB) * SCALE for ref in (x_ref, left_ref, right_ref))
    for i, y in enumerate((left, own, right)):
        anchor[1 + i] = y[0]
        store(0, OWN + (i - 1) * NB, y)
    load.wait()
    for t in range(FIRST):
        reach = HALO * (FIRST - 1 - t)
        y = step(0, OWN - reach, NB + 2 * reach)
        if t < FIRST - 1:
            store(0, OWN - reach, y)
        if t == 1:
            pl.semaphore_wait(barrier, len(near))
            relay(0)
            later = send(x_ref, got.at[0], 0, beside(-2))
            later.start()

    pack(raw.at[1], y)
    middle = [send(raw.at[1], got.at[1 + i], 1 + i, beside(d)) for i, d in enumerate((2, -2, 1, -1))]
    for c in middle:
        c.start()
    store(0, OWN, y)
    for c in middle:
        c.wait()
    relay(1)
    left2, right2, left, right = (got.at[1 + i] for i in range(4))
    reach = HALO * LAST - NB
    store(0, OWN - NB - reach, jnp.concatenate([rows(left2, NB - reach, NB), rows(left, 0, NB)], axis=0))
    store(0, OWN + NB, rows(right, 0, reach + 1))

    for s in range(1, LAST + 1):
        reach = HALO * (LAST - s)
        head = step(s - 1, OWN - reach, 2 * reach + 1)
        if s < LAST:
            store(s, OWN - reach, head)
    relay(2)

    row = lax.broadcasted_iota(jnp.int32, (8, BLOCK), 0)
    mine[...] = jnp.where(row < 3, head[0], 0.0)[0:4]
    for d in square:
        send(mine, plane.at[image], 7, in_plane(d)).start()

    later.wait()
    anchor[4] = rows(got.at[0], 0, 1)[0] * SCALE
    reach = HALO * LAST - NB
    store(0, OWN + NB + reach + 1, jnp.concatenate([rows(right, reach + 1, NB), rows(right2, 0, reach)], axis=0))

    def rest_of_step(s):
        lo = OWN + HALO * (LAST - s) + 1
        y = step(s - 1, lo, NB - 1)
        if s < LAST:
            store(s, lo, y)
        return y

    for s in range(1, LAST):
        rest_of_step(s)
    others = plane.at[pl.ds(1, IMAGES - 1)]
    pltpu.make_async_copy(others, others, sems.at[1, 7]).wait()
    plane[image] = mine[...]

    every = plane[...]
    change = every[1:] - every[:-1]
    change = jnp.concatenate([jnp.zeros((1, 4, BLOCK), F32), change], axis=0)
    squares = jnp.sum(jnp.sum(change * change, axis=1), axis=1, keepdims=True)
    at_row = lax.broadcasted_iota(jnp.int32, (IMAGES, BLOCK), 0)
    at_lane = lax.broadcasted_iota(jnp.int32, (IMAGES, BLOCK), 1)
    part[...] = jnp.sum(jnp.where(at_row == at_lane, squares, 0.0), axis=0, keepdims=True)

    relay(3)
    for d in ring:
        send(part, parts.at[slab], 10, beside(d)).start()
    pack(raw.at[0], jnp.concatenate([head, rest_of_step(LAST)], axis=0))
    images = [send(raw.at[0], around.at[i], 8 + i, across(d)) for i, d in enumerate((1, -1))]
    for c in images:
        c.start()
    for c in images:
        c.wait()
    pltpu.make_async_copy(others, others, sems.at[0, 7]).wait()
    rest = parts.at[pl.ds(1, N_SPACE - 1)]
    pltpu.make_async_copy(rest, rest, sems.at[1, 10]).wait()
    parts[slab] = part[...]

    total_ref[...] = jnp.sum(parts[...], axis=0)
    images_ref[0] = around[0]
    images_ref[1] = raw[0]
    images_ref[2] = around[1]
    pltpu.make_async_copy(rest, rest, sems.at[0, 10]).wait()


def blend(images_ref, total_ref, whole_ref, out_ref, fraction_ref, out, fraction, sems):
    image = lax.axis_index("image")
    lane = lax.broadcasted_iota(jnp.int32, (1, BLOCK), 1)
    lengths = jnp.sqrt(total_ref[...] * (1.0 / SCALE**2) + EPSILON)
    lengths = jnp.where((lane > 0) & (lane < IMAGES), lengths, 0.0)

    def arc(k):
        return jnp.sum(jnp.where(lane <= k, lengths, 0.0), axis=1, keepdims=True)

    full = arc(IMAGES - 1)
    fraction[...] = jnp.broadcast_to(arc(image) / full, (1, BLOCK))
    lower = whole_ref[NEIGHBOURS : NEIGHBOURS + 1, :BLOCK]
    code = whole_ref[NEIGHBOURS + 1 : NEIGHBOURS + 2, :BLOCK]
    arc_lower = arc(lower)
    place = lower.astype(F32) + code.astype(F32) / CODE_SCALE
    weight = (place / (IMAGES - 1) * full - arc_lower) / (arc(lower + 1) - arc_lower)
    earlier = lower < image
    for c in range(3):
        here = images_ref[1, c]
        below = jnp.where(earlier, images_ref[0, c], here)
        above = jnp.where(earlier, here, images_ref[2, c])
        out[c] = ((1.0 - weight) * below + weight * above) * (1.0 / SCALE)
    stores = [pltpu.make_async_copy(s, d, sems.at[i]) for i, (s, d) in enumerate([(out, out_ref), (fraction, fraction_ref)])]
    for c in stores:
        c.start()
    for c in stores:
        c.wait()


def body(positions, neighbours, brackets, codes):
    vmem = pl.BlockSpec(memory_space=pltpu.VMEM)
    left, right = (
        lax.ppermute(positions, "space", [(i, (i + d) % N_SPACE) for i in range(N_SPACE)]) for d in (1, -1)
    )
    along = [jnp.broadcast_to(v[:, None], (1, BLOCKS)) for v in (brackets, codes)]
    whole = jnp.concatenate([neighbours.T] + along, axis=0)
    images, total = pl.pallas_call(
        kernel,
        out_shape=(jax.ShapeDtypeStruct((3, 3, NB, BLOCK), F32), jax.ShapeDtypeStruct((1, BLOCK), F32)),
        in_specs=[vmem] * 4,
        out_specs=(vmem, vmem),
        scratch_shapes=[
            pltpu.SMEM((NEIGHBOURS + 2, BLOCKS), jnp.int32),
            pltpu.SemaphoreType.DMA,
            pltpu.SemaphoreType.REGULAR((3,)),
            pltpu.VMEM((LAST, EXT, 8, BLOCK), F32),
            pltpu.VMEM((EXT // NB, 8, BLOCK), F32),
            pltpu.VMEM((LAST, EXT, BLOCK, 48), BF16),
            pltpu.VMEM((LAST, EXT, 48, BLOCK), BF16),
            pltpu.VMEM((LAST, EXT, 32, BLOCK), BF16),
            pltpu.VMEM((2, 3, NB, BLOCK), F32),
            pltpu.VMEM((5, 3, NB, BLOCK), F32),
            pltpu.VMEM((2, 3, NB, BLOCK), F32),
            pltpu.VMEM((IMAGES, 4, BLOCK), F32),
            pltpu.VMEM((4, BLOCK), F32),
            pltpu.VMEM((1, BLOCK), F32),
            pltpu.VMEM((N_SPACE, 1, BLOCK), F32),
            pltpu.SemaphoreType.DMA((2, 11)),
        ],
        compiler_params=pltpu.CompilerParams(collective_id=0, has_side_effects=True, vmem_limit_bytes=48 << 20),
    )(*(x.reshape(3, NB, BLOCK) for x in (positions, left, right)), whole)
    hbm = pl.BlockSpec(memory_space=pl.ANY)
    out, fraction = pl.pallas_call(
        blend,
        out_shape=(jax.ShapeDtypeStruct((3, NB, BLOCK), F32), jax.ShapeDtypeStruct((1, BLOCK), F32)),
        in_specs=[vmem] * 3,
        out_specs=(hbm, hbm),
        scratch_shapes=[
            pltpu.VMEM((3, NB, BLOCK), F32),
            pltpu.VMEM((1, BLOCK), F32),
            pltpu.SemaphoreType.DMA((2,)),
        ],
        compiler_params=pltpu.CompilerParams(vmem_limit_bytes=16 << 20),
    )(images, total, whole)
    return out.reshape(1, 3, NB * BLOCK), fraction[0, :1]


def solution(mesh):
    placed = (P("image", None, "space"), P(), P("image"), P("image"))
    return jax.shard_map(
        body,
        mesh=mesh,
        in_specs=placed,
        out_specs=(P("image", None, "space"), P("image")),
        check_vma=False,
    )
```

```python
import functools
import math

import jax
import jax.numpy as jnp
from jax import lax
from jax.experimental import pallas as pl
from jax.experimental.pallas import tpu as pltpu
from jax.sharding import PartitionSpec as P

MESH = pl.DeviceIdType.MESH
F32, BF16 = jnp.float32, jnp.bfloat16

BLOCK = 128
HALO = 2
NB = 8
NEIGHBOURS = 3
IMAGES = 16
N_SPACE = 32
BLOCKS = NB * N_SPACE
TIME_STEP = 0.05
RESTRAINT = 1.0
COUPLING = 3.0
KERNEL_RATE = 0.125
EPSILON = 1e-06
CODE_SCALE = 65536.0

FIRST, LAST = 4, 6
OWN = 2 * NB
EXT = 5 * NB

SCALE = math.sqrt(KERNEL_RATE * math.log2(math.e))
PULL = TIME_STEP * COUPLING / (NEIGHBOURS * BLOCK)


def dot(a, b):
    return lax.dot_general(a, b, (((1,), (0,)), ((), ())), preferred_element_type=F32)


def split3(v):
    high = v.astype(BF16).astype(F32)
    rest = v - high
    middle = rest.astype(BF16).astype(F32)
    return high, middle, rest - middle


def operands(y):
    row = lax.broadcasted_iota(jnp.int32, y.shape, 1)
    y = jnp.where(row < 3, y, 0.0)
    square = jnp.sum(y * y, axis=1, keepdims=True)
    partner = jnp.where(row == 3, square, jnp.where(row == 4, 1.0, y))
    centre = jnp.where(row == 3, -1.0, jnp.where(row == 4, -square, y + y))
    ph, pm, plow = split3(partner)
    ch, cm, cl = split3(centre)
    a = jnp.concatenate([ph, ph, ph, pm, pm, plow], axis=1)
    b = jnp.concatenate([ch, cm, cl, ch, cm, ch], axis=1).astype(BF16)
    x = jnp.concatenate([ph, pm, plow, jnp.zeros_like(y)], axis=1).astype(BF16)
    return a, b, x


def kernel(
    x_ref, left_ref, right_ref, table_in, images_ref, total_ref,
    table, local_sem, relay_sems, cur, anchor, aop, bop, xop, raw, ahead, halves, far, whole, around, plane, mine, part, parts, sems,
):
    image, slab = lax.axis_index("image"), lax.axis_index("space")

    def beside(d):
        return (image, lax.rem(slab + d + N_SPACE, N_SPACE))

    def across(d):
        return (lax.rem(image + d + IMAGES, IMAGES), slab)

    ring = sorted(range(1, N_SPACE), key=lambda d: -min(d, N_SPACE - d))
    square = [(dx, dy) for dx in range(4) for dy in range(4) if (dx, dy) != (0, 0)]
    square.sort(key=lambda d: -sum(min(v, 4 - v) for v in d))

    def in_plane(d):
        return (lax.rem(image // 4 + d[0], 4) * 4 + lax.rem(lax.rem(image, 4) + d[1], 4), slab)

    def greet(semaphore, peers):
        for peer in peers:
            pl.semaphore_signal(semaphore, inc=1, device_id=peer, device_id_type=MESH)

    barrier = pltpu.get_barrier_semaphore()
    near = [peer for d in (1, -1, 2, -2) for peer in (beside(d), across(d))]
    stages = [
        [peer for d in (2, -2) for peer in (beside(d), across(d))],
        [peer for d in (4, -4) for peer in (beside(d), across(d))],
        [beside(8), beside(-8)],
    ]

    def relay(j):
        if j > 0:
            pl.semaphore_wait(relay_sems.at[j - 1], len(stages[j - 1]))
        if j < len(stages):
            greet(relay_sems.at[j], stages[j])

    greet(barrier, near)
    load = pltpu.make_async_copy(table_in, table, local_sem)
    load.start()

    def store(version, lo, y):
        a, b, x = operands(y)
        n = y.shape[0]
        cur[version, lo : lo + n] = y
        bop[version, lo : lo + n] = b
        xop[version, lo : lo + n] = x
        for i in range(n):
            aop[version, lo + i] = a[i].T.astype(BF16)

    def rows(slab_ref, first, last):
        n = last - first
        coordinates = [slab_ref[c, first:last].reshape(n, 1, BLOCK) for c in range(3)]
        return jnp.concatenate(coordinates + [jnp.zeros((n, 5, BLOCK), F32)], axis=1)

    def send(source, target, slot, peer):
        return pltpu.make_async_remote_copy(
            src_ref=source, dst_ref=target, send_sem=sems.at[0, slot], recv_sem=sems.at[1, slot],
            device_id=peer, device_id_type=MESH,
        )

    def step(version, *runs):
        blocks = [e for lo, n in runs for e in range(lo, lo + n)]
        first = slab * NB + BLOCKS - OWN
        partners = [
            [e - HALO + table[k, lax.rem(first + e, BLOCKS)] for k in range(NEIGHBOURS)]
            for e in blocks
        ]
        weights = []
        for e, ps in zip(blocks, partners):
            exponent = dot(jnp.concatenate([aop[version, p] for p in ps], axis=0), bop[version, e])
            w = jnp.exp2(exponent)
            high = w.astype(BF16)
            weights.append(jnp.concatenate([high, (w - high.astype(F32)).astype(BF16)], axis=0))
        sums = []
        for ps, w in zip(partners, weights):
            x = jnp.concatenate([xop[version, p] for p in ps], axis=1)
            total = dot(jnp.concatenate([x, x], axis=1), w)
            sums.append(total[0:8] + total[8:16] + total[16:24])
        held = [cur[version, lo : lo + n] for lo, n in runs]
        y = jnp.concatenate(held, axis=0) if len(runs) > 1 else held[0]
        total = jnp.stack(sums, axis=0)
        y_new = y + PULL * (y * total[:, 4:5] - total)
        held = [
            y_new[i : i + 1] - (TIME_STEP * RESTRAINT) * (y[i : i + 1] - anchor[e // NB][None])
            if e % NB == 0
            else y_new[i : i + 1]
            for i, e in enumerate(blocks)
        ]
        return jnp.concatenate(held, axis=0) if len(held) > 1 else held[0]

    def pack(ref, y):
        for c in range(3):
            ref[c] = y[:, c]

    own, left, right = (rows(ref, 0, NB) * SCALE for ref in (x_ref, left_ref, right_ref))
    for i, y in enumerate((left, own, right)):
        anchor[1 + i] = y[0]
        store(0, OWN + (i - 1) * NB, y)
    load.wait()
    for t in range(FIRST):
        reach = HALO * (FIRST - 1 - t)
        y = step(0, (OWN - reach, NB + 2 * reach))
        if t < FIRST - 1:
            store(0, OWN - reach, y)
        if t == 1:
            pl.semaphore_wait(barrier, len(near))
            relay(0)
            later = send(x_ref, ahead, 0, beside(-2))
            later.start()

    for h in range(2):
        pack(halves.at[h], y[h * NB // 2 : (h + 1) * NB // 2])
    left2, left, right, right2 = far.at[0], whole.at[0], whole.at[1], far.at[1]
    middle = [
        send(halves.at[1], left2, 1, beside(2)),
        send(halves, left, 2, beside(1)),
        send(halves, right, 3, beside(-1)),
    ]
    for c in middle:
        c.start()
    last = send(halves.at[0], right2, 4, beside(-2))
    last.start()
    store(0, OWN, y)
    inner = (OWN + HALO, NB - 2 * HALO)
    store(1, inner[0], step(0, inner))
    for c in middle:
        c.wait()
    relay(1)
    left = jnp.concatenate([rows(left2, 0, NB // 2)] + [rows(left.at[h], 0, NB // 2) for h in range(2)], axis=0)
    store(0, OWN - NB - NB // 2, left)
    store(0, OWN + NB, jnp.concatenate([rows(right.at[0], 0, NB // 2), rows(right.at[1], 0, 1)], axis=0))

    for s in range(1, LAST + 1):
        reach = HALO * (LAST - s)
        lo, end = OWN - reach, OWN + reach + 1
        if s == 1:
            n = inner[0] - lo
            after = inner[0] + inner[1]
            head = step(0, (lo, n), (after, end - after))
            store(1, lo, head[:n])
            store(1, after, head[n:])
            continue
        head = step(s - 1, (lo, end - lo))
        if s < LAST:
            store(s, lo, head)
        if s == 4:
            relay(2)

    row = lax.broadcasted_iota(jnp.int32, (8, BLOCK), 0)
    mine[...] = jnp.where(row < 3, head[0], 0.0)[0:4]
    for d in square:
        send(mine, plane.at[image], 7, in_plane(d)).start()

    later.wait()
    anchor[4] = rows(ahead, 0, 1)[0] * SCALE
    last.wait()
    store(0, OWN + NB + NB // 2 + 1, jnp.concatenate([rows(right.at[1], 1, NB // 2), rows(right2, 0, NB // 2)], axis=0))

    def rest_of_step(s):
        lo = OWN + HALO * (LAST - s) + 1
        y = step(s - 1, (lo, NB - 1))
        if s < LAST:
            store(s, lo, y)
        return y

    for s in range(1, LAST - 1):
        rest_of_step(s)
    others = plane.at[pl.ds(1, IMAGES - 1)]
    pltpu.make_async_copy(others, others, sems.at[1, 7]).wait()
    plane[image] = mine[...]

    every = plane[...]
    change = every[1:] - every[:-1]
    change = jnp.concatenate([jnp.zeros((1, 4, BLOCK), F32), change], axis=0)
    squares = jnp.sum(jnp.sum(change * change, axis=1), axis=1, keepdims=True)
    at_row = lax.broadcasted_iota(jnp.int32, (IMAGES, BLOCK), 0)
    at_lane = lax.broadcasted_iota(jnp.int32, (IMAGES, BLOCK), 1)
    part[...] = jnp.sum(jnp.where(at_row == at_lane, squares, 0.0), axis=0, keepdims=True)

    relay(3)
    for d in ring:
        send(part, parts.at[slab], 10, beside(d)).start()
    rest_of_step(LAST - 1)
    pack(raw, jnp.concatenate([head, rest_of_step(LAST)], axis=0))
    images = [send(raw, around.at[i], 8 + i, across(d)) for i, d in enumerate((1, -1))]
    for c in images:
        c.start()
    for c in images:
        c.wait()
    pltpu.make_async_copy(others, others, sems.at[0, 7]).wait()
    rest = parts.at[pl.ds(1, N_SPACE - 1)]
    pltpu.make_async_copy(rest, rest, sems.at[1, 10]).wait()
    parts[slab] = part[...]

    total_ref[...] = jnp.sum(parts[...], axis=0)
    images_ref[0] = around[0]
    images_ref[1] = raw[...]
    images_ref[2] = around[1]
    pltpu.make_async_copy(rest, rest, sems.at[0, 10]).wait()


def blend(images_ref, total_ref, whole_ref, out_ref, fraction_ref, out, fraction, sems):
    image = lax.axis_index("image")
    lane = lax.broadcasted_iota(jnp.int32, (1, BLOCK), 1)
    lengths = jnp.sqrt(total_ref[...] * (1.0 / SCALE**2) + EPSILON)
    lengths = jnp.where((lane > 0) & (lane < IMAGES), lengths, 0.0)

    def arc(k):
        return jnp.sum(jnp.where(lane <= k, lengths, 0.0), axis=1, keepdims=True)

    full = arc(IMAGES - 1)
    fraction[...] = jnp.broadcast_to(arc(image) / full, (1, BLOCK))
    lower = whole_ref[NEIGHBOURS : NEIGHBOURS + 1, :BLOCK]
    code = whole_ref[NEIGHBOURS + 1 : NEIGHBOURS + 2, :BLOCK]
    arc_lower = arc(lower)
    place = lower.astype(F32) + code.astype(F32) / CODE_SCALE
    weight = (place / (IMAGES - 1) * full - arc_lower) / (arc(lower + 1) - arc_lower)
    earlier = lower < image
    for c in range(3):
        here = images_ref[1, c]
        below = jnp.where(earlier, images_ref[0, c], here)
        above = jnp.where(earlier, here, images_ref[2, c])
        out[c] = ((1.0 - weight) * below + weight * above) * (1.0 / SCALE)
    stores = [pltpu.make_async_copy(s, d, sems.at[i]) for i, (s, d) in enumerate([(out, out_ref), (fraction, fraction_ref)])]
    for c in stores:
        c.start()
    for c in stores:
        c.wait()


def body(positions, neighbours, brackets, codes):
    vmem = pl.BlockSpec(memory_space=pltpu.VMEM)
    left, right = (
        lax.ppermute(positions, "space", [(i, (i + d) % N_SPACE) for i in range(N_SPACE)]) for d in (1, -1)
    )
    along = [jnp.broadcast_to(v[:, None], (1, BLOCKS)) for v in (brackets, codes)]
    whole = jnp.concatenate([neighbours.T] + along, axis=0)
    images, total = pl.pallas_call(
        kernel,
        out_shape=(jax.ShapeDtypeStruct((3, 3, NB, BLOCK), F32), jax.ShapeDtypeStruct((1, BLOCK), F32)),
        in_specs=[vmem] * 4,
        out_specs=(vmem, vmem),
        scratch_shapes=[
            pltpu.SMEM((NEIGHBOURS + 2, BLOCKS), jnp.int32),
            pltpu.SemaphoreType.DMA,
            pltpu.SemaphoreType.REGULAR((3,)),
            pltpu.VMEM((LAST, EXT, 8, BLOCK), F32),
            pltpu.VMEM((EXT // NB, 8, BLOCK), F32),
            pltpu.VMEM((LAST, EXT, BLOCK, 48), BF16),
            pltpu.VMEM((LAST, EXT, 48, BLOCK), BF16),
            pltpu.VMEM((LAST, EXT, 32, BLOCK), BF16),
            pltpu.VMEM((3, NB, BLOCK), F32),
            pltpu.VMEM((3, NB, BLOCK), F32),
            pltpu.VMEM((2, 3, NB // 2, BLOCK), F32),
            pltpu.VMEM((2, 3, NB // 2, BLOCK), F32),
            pltpu.VMEM((2, 2, 3, NB // 2, BLOCK), F32),
            pltpu.VMEM((2, 3, NB, BLOCK), F32),
            pltpu.VMEM((IMAGES, 4, BLOCK), F32),
            pltpu.VMEM((4, BLOCK), F32),
            pltpu.VMEM((1, BLOCK), F32),
            pltpu.VMEM((N_SPACE, 1, BLOCK), F32),
            pltpu.SemaphoreType.DMA((2, 11)),
        ],
        compiler_params=pltpu.CompilerParams(collective_id=0, has_side_effects=True, vmem_limit_bytes=48 << 20),
    )(*(x.reshape(3, NB, BLOCK) for x in (positions, left, right)), whole)
    hbm = pl.BlockSpec(memory_space=pl.ANY)
    out, fraction = pl.pallas_call(
        blend,
        out_shape=(jax.ShapeDtypeStruct((3, NB, BLOCK), F32), jax.ShapeDtypeStruct((1, BLOCK), F32)),
        in_specs=[vmem] * 3,
        out_specs=(hbm, hbm),
        scratch_shapes=[
            pltpu.VMEM((3, NB, BLOCK), F32),
            pltpu.VMEM((1, BLOCK), F32),
            pltpu.SemaphoreType.DMA((2,)),
        ],
        compiler_params=pltpu.CompilerParams(vmem_limit_bytes=16 << 20),
    )(images, total, whole)
    return out.reshape(1, 3, NB * BLOCK), fraction[0, :1]


def solution(mesh):
    placed = (P("image", None, "space"), P(), P("image"), P("image"))
    return jax.shard_map(
        body,
        mesh=mesh,
        in_specs=placed,
        out_specs=(P("image", None, "space"), P("image")),
        check_vma=False,
    )
```

```python
import functools
import math

import jax
import jax.numpy as jnp
from jax import lax
from jax.experimental import pallas as pl
from jax.experimental.pallas import tpu as pltpu
from jax.sharding import PartitionSpec as P

MESH = pl.DeviceIdType.MESH
F32, BF16 = jnp.float32, jnp.bfloat16

BLOCK = 128
HALO = 2
NB = 8
NEIGHBOURS = 3
IMAGES = 16
N_SPACE = 32
BLOCKS = NB * N_SPACE
TIME_STEP = 0.05
RESTRAINT = 1.0
COUPLING = 3.0
KERNEL_RATE = 0.125
EPSILON = 1e-06
CODE_SCALE = 65536.0

FIRST, LAST = 4, 6
OWN = 2 * NB
EXT = 5 * NB

SCALE = math.sqrt(KERNEL_RATE * math.log2(math.e))
PULL = TIME_STEP * COUPLING / (NEIGHBOURS * BLOCK)


def dot(a, b):
    return lax.dot_general(a, b, (((1,), (0,)), ((), ())), preferred_element_type=F32)


def split3(v):
    high = v.astype(BF16).astype(F32)
    rest = v - high
    middle = rest.astype(BF16).astype(F32)
    return high, middle, rest - middle


def operands(y):
    row = lax.broadcasted_iota(jnp.int32, y.shape, 1)
    y = jnp.where(row < 3, y, 0.0)
    square = jnp.sum(y * y, axis=1, keepdims=True)
    partner = jnp.where(row == 3, square, jnp.where(row == 4, 1.0, y))
    centre = jnp.where(row == 3, -1.0, jnp.where(row == 4, -square, y + y))
    ph, pm, plow = split3(partner)
    ch, cm, cl = split3(centre)
    a = jnp.concatenate([ph, ph, ph, pm, pm, plow], axis=1).astype(BF16)
    b = jnp.concatenate([ch, cm, cl, ch, cm, ch], axis=1).astype(BF16)
    x = jnp.concatenate([ph, pm, plow, jnp.zeros_like(y)], axis=1).astype(BF16)
    return a, b, x


def kernel(
    x_ref, beside_ref, apart_ref, table_in, images_ref, total_ref,
    table, local_sem, relay_sems, cur, anchor, aop, bop, xop, raw, ahead, halves, far, whole, around, plane, mine, part, parts, sems,
):
    image, slab = lax.axis_index("image"), lax.axis_index("space")

    def beside(d):
        return (image, lax.rem(slab + d + N_SPACE, N_SPACE))

    def across(d):
        return (lax.rem(image + d + IMAGES, IMAGES), slab)

    ring = sorted(range(1, N_SPACE), key=lambda d: -min(d, N_SPACE - d))
    square = [(dx, dy) for dx in range(4) for dy in range(4) if (dx, dy) != (0, 0)]
    square.sort(key=lambda d: -sum(min(v, 4 - v) for v in d))

    def in_plane(d):
        return (lax.rem(image // 4 + d[0], 4) * 4 + lax.rem(lax.rem(image, 4) + d[1], 4), slab)

    def greet(semaphore, peers):
        for peer in peers:
            pl.semaphore_signal(semaphore, inc=1, device_id=peer, device_id_type=MESH)

    barrier = pltpu.get_barrier_semaphore()
    near = [peer for d in (1, -1, 2, -2) for peer in (beside(d), across(d))]
    stages = [
        [peer for d in (2, -2) for peer in (beside(d), across(d))],
        [peer for d in (4, -4) for peer in (beside(d), across(d))],
        [beside(8), beside(-8)],
    ]

    def relay(j):
        if j > 0:
            pl.semaphore_wait(relay_sems.at[j - 1], len(stages[j - 1]))
        if j < len(stages):
            greet(relay_sems.at[j], stages[j])

    greet(barrier, near)
    load = pltpu.make_async_copy(table_in, table, local_sem)
    load.start()

    def store(version, lo, y):
        a, b, x = operands(y)
        n = y.shape[0]
        cur[version, lo : lo + n] = y
        bop[version, lo : lo + n] = b
        xop[version, lo : lo + n] = x
        for i in range(n):
            aop[version, lo + i] = a[i].T

    def rows(slab_ref, first, last):
        n = last - first
        coordinates = [slab_ref[c, first:last].reshape(n, 1, BLOCK) for c in range(3)]
        return jnp.concatenate(coordinates + [jnp.zeros((n, 5, BLOCK), F32)], axis=1)

    def send(source, target, slot, peer):
        return pltpu.make_async_remote_copy(
            src_ref=source, dst_ref=target, send_sem=sems.at[0, slot], recv_sem=sems.at[1, slot],
            device_id=peer, device_id_type=MESH,
        )

    def step(version, *runs):
        blocks = [e for lo, n in runs for e in range(lo, lo + n)]
        first = slab * NB + BLOCKS - OWN
        partners = [
            [e - HALO + table[k, lax.rem(first + e, BLOCKS)] for k in range(NEIGHBOURS)]
            for e in blocks
        ]
        weights = []
        for e, ps in zip(blocks, partners):
            exponent = dot(jnp.concatenate([aop[version, p] for p in ps], axis=0), bop[version, e])
            w = jnp.exp2(exponent)
            high = w.astype(BF16)
            weights.append(jnp.concatenate([high, (w - high.astype(F32)).astype(BF16)], axis=0))
        sums = []
        for ps, w in zip(partners, weights):
            x = jnp.concatenate([xop[version, p] for p in ps], axis=1)
            total = dot(jnp.concatenate([x, x], axis=1), w)
            sums.append(total[0:8] + total[8:16] + total[16:24])
        held = [cur[version, lo : lo + n] for lo, n in runs]
        y = jnp.concatenate(held, axis=0) if len(runs) > 1 else held[0]
        total = jnp.stack(sums, axis=0)
        y_new = y + PULL * (y * total[:, 4:5] - total)
        held = [
            y_new[i : i + 1] - (TIME_STEP * RESTRAINT) * (y[i : i + 1] - anchor[e // NB][None])
            if e % NB == 0
            else y_new[i : i + 1]
            for i, e in enumerate(blocks)
        ]
        return jnp.concatenate(held, axis=0) if len(held) > 1 else held[0]

    def pack(ref, y):
        for c in range(3):
            ref[c] = y[:, c]

    own, apart, partner = (rows(ref, 0, NB) * SCALE for ref in (x_ref, apart_ref, beside_ref))
    second = lax.rem(slab, 2) == 1
    left = jnp.where(second, partner, apart)
    right = jnp.where(second, apart, partner)
    for i, y in enumerate((left, own, right)):
        anchor[1 + i] = y[0]
        store(0, OWN + (i - 1) * NB, y)
    load.wait()
    for t in range(FIRST):
        reach = HALO * (FIRST - 1 - t)
        y = step(0, (OWN - reach, NB + 2 * reach))
        if t < FIRST - 1:
            store(0, OWN - reach, y)
        if t == 1:
            pl.semaphore_wait(barrier, len(near))
            relay(0)
            later = send(x_ref, ahead, 0, beside(-2))
            later.start()

    for h in range(2):
        pack(halves.at[h], y[h * NB // 2 : (h + 1) * NB // 2])
    left2, left, right, right2 = far.at[0], whole.at[0], whole.at[1], far.at[1]
    middle = [
        send(halves.at[1], left2, 1, beside(2)),
        send(halves, left, 2, beside(1)),
        send(halves, right, 3, beside(-1)),
    ]
    for c in middle:
        c.start()
    last = send(halves.at[0], right2, 4, beside(-2))
    last.start()
    store(0, OWN, y)
    inner = (OWN + HALO, NB - 2 * HALO)
    store(1, inner[0], step(0, inner))
    for c in middle:
        c.wait()
    relay(1)
    left = jnp.concatenate([rows(left2, 0, NB // 2)] + [rows(left.at[h], 0, NB // 2) for h in range(2)], axis=0)
    store(0, OWN - NB - NB // 2, left)
    store(0, OWN + NB, jnp.concatenate([rows(right.at[0], 0, NB // 2), rows(right.at[1], 0, 1)], axis=0))

    for s in range(1, LAST + 1):
        reach = HALO * (LAST - s)
        lo, end = OWN - reach, OWN + reach + 1
        if s == 1:
            n = inner[0] - lo
            after = inner[0] + inner[1]
            head = step(0, (lo, n), (after, end - after))
            store(1, lo, head[:n])
            store(1, after, head[n:])
            continue
        head = step(s - 1, (lo, end - lo))
        if s < LAST:
            store(s, lo, head)
        if s == 4:
            relay(2)

    row = lax.broadcasted_iota(jnp.int32, (8, BLOCK), 0)
    mine[...] = jnp.where(row < 3, head[0], 0.0)[0:4]
    for d in square:
        send(mine, plane.at[image], 7, in_plane(d)).start()

    later.wait()
    anchor[4] = rows(ahead, 0, 1)[0] * SCALE
    last.wait()
    store(0, OWN + NB + NB // 2 + 1, jnp.concatenate([rows(right.at[1], 1, NB // 2), rows(right2, 0, NB // 2)], axis=0))

    def rest_of_step(s):
        lo = OWN + HALO * (LAST - s) + 1
        y = step(s - 1, (lo, NB - 1))
        if s < LAST:
            store(s, lo, y)
        return y

    for s in range(1, LAST - 1):
        rest_of_step(s)
    others = plane.at[pl.ds(1, IMAGES - 1)]
    pltpu.make_async_copy(others, others, sems.at[1, 7]).wait()
    plane[image] = mine[...]

    every = plane[...]
    change = every[1:] - every[:-1]
    change = jnp.concatenate([jnp.zeros((1, 4, BLOCK), F32), change], axis=0)
    squares = jnp.sum(jnp.sum(change * change, axis=1), axis=1, keepdims=True)
    at_row = lax.broadcasted_iota(jnp.int32, (IMAGES, BLOCK), 0)
    at_lane = lax.broadcasted_iota(jnp.int32, (IMAGES, BLOCK), 1)
    part[...] = jnp.sum(jnp.where(at_row == at_lane, squares, 0.0), axis=0, keepdims=True)

    relay(3)
    for d in ring:
        send(part, parts.at[slab], 10, beside(d)).start()
    rest_of_step(LAST - 1)
    pack(raw, jnp.concatenate([head, rest_of_step(LAST)], axis=0))
    images = [send(raw, around.at[i], 8 + i, across(d)) for i, d in enumerate((1, -1))]
    for c in images:
        c.start()
    for c in images:
        c.wait()
    pltpu.make_async_copy(others, others, sems.at[0, 7]).wait()
    rest = parts.at[pl.ds(1, N_SPACE - 1)]
    pltpu.make_async_copy(rest, rest, sems.at[1, 10]).wait()
    parts[slab] = part[...]

    total_ref[...] = jnp.sum(parts[...], axis=0)
    images_ref[0] = around[0]
    images_ref[1] = raw[...]
    images_ref[2] = around[1]
    pltpu.make_async_copy(rest, rest, sems.at[0, 10]).wait()


def blend(images_ref, total_ref, whole_ref, out_ref, fraction_ref, out, fraction, sems):
    image = lax.axis_index("image")
    lane = lax.broadcasted_iota(jnp.int32, (1, BLOCK), 1)
    lengths = jnp.sqrt(total_ref[...] * (1.0 / SCALE**2) + EPSILON)
    lengths = jnp.where((lane > 0) & (lane < IMAGES), lengths, 0.0)

    def arc(k):
        return jnp.sum(jnp.where(lane <= k, lengths, 0.0), axis=1, keepdims=True)

    full = arc(IMAGES - 1)
    fraction[...] = jnp.broadcast_to(arc(image) / full, (1, BLOCK))
    lower = whole_ref[NEIGHBOURS : NEIGHBOURS + 1, :BLOCK]
    code = whole_ref[NEIGHBOURS + 1 : NEIGHBOURS + 2, :BLOCK]
    arc_lower = arc(lower)
    place = lower.astype(F32) + code.astype(F32) / CODE_SCALE
    weight = (place / (IMAGES - 1) * full - arc_lower) / (arc(lower + 1) - arc_lower)
    earlier = lower < image
    for c in range(3):
        here = images_ref[1, c]
        below = jnp.where(earlier, images_ref[0, c], here)
        above = jnp.where(earlier, here, images_ref[2, c])
        out[c] = ((1.0 - weight) * below + weight * above) * (1.0 / SCALE)
    stores = [pltpu.make_async_copy(s, d, sems.at[i]) for i, (s, d) in enumerate([(out, out_ref), (fraction, fraction_ref)])]
    for c in stores:
        c.start()
    for c in stores:
        c.wait()


def body(positions, neighbours, brackets, codes):
    vmem = pl.BlockSpec(memory_space=pltpu.VMEM)
    partner = lax.ppermute(positions, "space", [(i, i + 1 - 2 * (i % 2)) for i in range(N_SPACE)])
    apart = lax.ppermute(positions, "space", [(i, (i + 2 * (i % 2) - 1) % N_SPACE) for i in range(N_SPACE)])
    along = [jnp.broadcast_to(v[:, None], (1, BLOCKS)) for v in (brackets, codes)]
    whole = jnp.concatenate([neighbours.T] + along, axis=0)
    images, total = pl.pallas_call(
        kernel,
        out_shape=(jax.ShapeDtypeStruct((3, 3, NB, BLOCK), F32), jax.ShapeDtypeStruct((1, BLOCK), F32)),
        in_specs=[vmem] * 4,
        out_specs=(vmem, vmem),
        scratch_shapes=[
            pltpu.SMEM((NEIGHBOURS + 2, BLOCKS), jnp.int32),
            pltpu.SemaphoreType.DMA,
            pltpu.SemaphoreType.REGULAR((3,)),
            pltpu.VMEM((LAST, EXT, 8, BLOCK), F32),
            pltpu.VMEM((EXT // NB, 8, BLOCK), F32),
            pltpu.VMEM((LAST, EXT, BLOCK, 48), BF16),
            pltpu.VMEM((LAST, EXT, 48, BLOCK), BF16),
            pltpu.VMEM((LAST, EXT, 32, BLOCK), BF16),
            pltpu.VMEM((3, NB, BLOCK), F32),
            pltpu.VMEM((3, NB, BLOCK), F32),
            pltpu.VMEM((2, 3, NB // 2, BLOCK), F32),
            pltpu.VMEM((2, 3, NB // 2, BLOCK), F32),
            pltpu.VMEM((2, 2, 3, NB // 2, BLOCK), F32),
            pltpu.VMEM((2, 3, NB, BLOCK), F32),
            pltpu.VMEM((IMAGES, 4, BLOCK), F32),
            pltpu.VMEM((4, BLOCK), F32),
            pltpu.VMEM((1, BLOCK), F32),
            pltpu.VMEM((N_SPACE, 1, BLOCK), F32),
            pltpu.SemaphoreType.DMA((2, 11)),
        ],
        compiler_params=pltpu.CompilerParams(collective_id=0, has_side_effects=True, vmem_limit_bytes=48 << 20),
    )(*(x.reshape(3, NB, BLOCK) for x in (positions, partner, apart)), whole)
    hbm = pl.BlockSpec(memory_space=pl.ANY)
    out, fraction = pl.pallas_call(
        blend,
        out_shape=(jax.ShapeDtypeStruct((3, NB, BLOCK), F32), jax.ShapeDtypeStruct((1, BLOCK), F32)),
        in_specs=[vmem] * 3,
        out_specs=(hbm, hbm),
        scratch_shapes=[
            pltpu.VMEM((3, NB, BLOCK), F32),
            pltpu.VMEM((1, BLOCK), F32),
            pltpu.SemaphoreType.DMA((2,)),
        ],
        compiler_params=pltpu.CompilerParams(vmem_limit_bytes=16 << 20),
    )(images, total, whole)
    return out.reshape(1, 3, NB * BLOCK), fraction[0, :1]


def solution(mesh):
    placed = (P("image", None, "space"), P(), P("image"), P("image"))
    return jax.shard_map(
        body,
        mesh=mesh,
        in_specs=placed,
        out_specs=(P("image", None, "space"), P("image")),
        check_vma=False,
    )
```

```python
import functools
import math

import jax
import jax.numpy as jnp
from jax import lax
from jax.experimental import pallas as pl
from jax.experimental.pallas import tpu as pltpu
from jax.sharding import PartitionSpec as P

MESH = pl.DeviceIdType.MESH
F32, BF16 = jnp.float32, jnp.bfloat16

BLOCK = 128
HALO = 2
NB = 8
NEIGHBOURS = 3
IMAGES = 16
N_SPACE = 32
BLOCKS = NB * N_SPACE
TIME_STEP = 0.05
RESTRAINT = 1.0
COUPLING = 3.0
KERNEL_RATE = 0.125
EPSILON = 1e-06
CODE_SCALE = 65536.0

FIRST, LAST = 4, 6
OWN = 2 * NB
EXT = 5 * NB

SCALE = math.sqrt(KERNEL_RATE * math.log2(math.e))
PULL = TIME_STEP * COUPLING / (NEIGHBOURS * BLOCK)


def dot(a, b):
    return lax.dot_general(a, b, (((1,), (0,)), ((), ())), preferred_element_type=F32)


def split3(v):
    high = v.astype(BF16).astype(F32)
    rest = v - high
    middle = rest.astype(BF16).astype(F32)
    return high, middle, rest - middle


def operands(y):
    row = lax.broadcasted_iota(jnp.int32, y.shape, 1)
    y = jnp.where(row < 3, y, 0.0)
    square = jnp.sum(y * y, axis=1, keepdims=True)
    partner = jnp.where(row == 3, square, jnp.where(row == 4, 1.0, y))
    centre = jnp.where(row == 3, -1.0, jnp.where(row == 4, -square, y + y))
    ph, pm, plow = split3(partner)
    ch, cm, cl = split3(centre)
    a = jnp.concatenate([ph, ph, ph, pm, pm, plow], axis=1).astype(BF16)
    b = jnp.concatenate([ch, cm, cl, ch, cm, ch], axis=1).astype(BF16)
    x = jnp.concatenate([ph, pm, plow, jnp.zeros_like(y)], axis=1).astype(BF16)
    return a, b, x


def kernel(
    x_ref, left_ref, right_ref, table_in, images_ref, total_ref,
    table, local_sem, relay_sems, cur, anchor, aop, bop, xop, raw, ahead, halves, far, whole, around, plane, mine, part, parts, sems,
):
    image, slab = lax.axis_index("image"), lax.axis_index("space")

    def beside(d):
        return (image, lax.rem(slab + d + N_SPACE, N_SPACE))

    def across(d):
        return (lax.rem(image + d + IMAGES, IMAGES), slab)

    ring = sorted(range(1, N_SPACE), key=lambda d: -min(d, N_SPACE - d))
    square = [(dx, dy) for dx in range(4) for dy in range(4) if (dx, dy) != (0, 0)]
    square.sort(key=lambda d: -sum(min(v, 4 - v) for v in d))

    def in_plane(d):
        return (lax.rem(image // 4 + d[0], 4) * 4 + lax.rem(lax.rem(image, 4) + d[1], 4), slab)

    def greet(semaphore, peers):
        for peer in peers:
            pl.semaphore_signal(semaphore, inc=1, device_id=peer, device_id_type=MESH)

    barrier = pltpu.get_barrier_semaphore()
    near = [peer for d in (1, -1, 2, -2) for peer in (beside(d), across(d))]
    stages = [
        [peer for d in (2, -2) for peer in (beside(d), across(d))],
        [peer for d in (4, -4) for peer in (beside(d), across(d))],
        [beside(8), beside(-8)],
    ]

    def relay(j):
        if j > 0:
            pl.semaphore_wait(relay_sems.at[j - 1], len(stages[j - 1]))
        if j < len(stages):
            greet(relay_sems.at[j], stages[j])

    greet(barrier, near)
    load = pltpu.make_async_copy(table_in, table, local_sem)
    load.start()

    def store(version, lo, y):
        a, b, x = operands(y)
        n = y.shape[0]
        cur[version, lo : lo + n] = y
        bop[version, lo : lo + n] = b
        xop[version, lo : lo + n] = x
        for i in range(n):
            aop[version, lo + i] = a[i].T

    def rows(slab_ref, first, last):
        n = last - first
        coordinates = [slab_ref[c, first:last].reshape(n, 1, BLOCK) for c in range(3)]
        return jnp.concatenate(coordinates + [jnp.zeros((n, 5, BLOCK), F32)], axis=1)

    def send(source, target, slot, peer):
        return pltpu.make_async_remote_copy(
            src_ref=source, dst_ref=target, send_sem=sems.at[0, slot], recv_sem=sems.at[1, slot],
            device_id=peer, device_id_type=MESH,
        )

    def step(version, *runs):
        blocks = [e for lo, n in runs for e in range(lo, lo + n)]
        first = slab * NB + BLOCKS - OWN
        partners = [
            [e - HALO + table[k, lax.rem(first + e, BLOCKS)] for k in range(NEIGHBOURS)]
            for e in blocks
        ]
        weights = []
        for e, ps in zip(blocks, partners):
            exponent = dot(jnp.concatenate([aop[version, p] for p in ps], axis=0), bop[version, e])
            w = jnp.exp2(exponent)
            high = w.astype(BF16)
            weights.append(jnp.concatenate([high, (w - high.astype(F32)).astype(BF16)], axis=0))
        sums = []
        for ps, w in zip(partners, weights):
            x = jnp.concatenate([xop[version, p] for p in ps], axis=1)
            total = dot(jnp.concatenate([x, x], axis=1), w)
            sums.append(total[0:8] + total[8:16] + total[16:24])
        held = [cur[version, lo : lo + n] for lo, n in runs]
        y = jnp.concatenate(held, axis=0) if len(runs) > 1 else held[0]
        total = jnp.stack(sums, axis=0)
        y_new = y + PULL * (y * total[:, 4:5] - total)
        held = [
            y_new[i : i + 1] - (TIME_STEP * RESTRAINT) * (y[i : i + 1] - anchor[e // NB][None])
            if e % NB == 0
            else y_new[i : i + 1]
            for i, e in enumerate(blocks)
        ]
        return jnp.concatenate(held, axis=0) if len(held) > 1 else held[0]

    def pack(ref, y):
        for c in range(3):
            ref[c] = y[:, c]

    own, left, right = (rows(ref, 0, NB) * SCALE for ref in (x_ref, left_ref, right_ref))
    for i, y in enumerate((left, own, right)):
        anchor[1 + i] = y[0]
        store(0, OWN + (i - 1) * NB, y)
    load.wait()
    for t in range(FIRST):
        reach = HALO * (FIRST - 1 - t)
        y = step(0, (OWN - reach, NB + 2 * reach))
        if t < FIRST - 1:
            store(0, OWN - reach, y)
        if t == 1:
            pl.semaphore_wait(barrier, len(near))
            relay(0)
            later = send(x_ref, ahead, 0, beside(-2))
            later.start()

    for h in range(2):
        pack(halves.at[h], y[h * NB // 2 : (h + 1) * NB // 2])
    left2, left, right, right2 = far.at[0], whole.at[0], whole.at[1], far.at[1]
    middle = [
        send(halves.at[1], left2, 1, beside(2)),
        send(halves, left, 2, beside(1)),
        send(halves, right, 3, beside(-1)),
    ]
    for c in middle:
        c.start()
    last = send(halves.at[0], right2, 4, beside(-2))
    last.start()
    store(0, OWN, y)

    def advance(version, *runs):
        y = step(version, *runs)
        at = 0
        for lo, n in runs:
            store(version + 1, lo, y[at : at + n])
            at += n

    def take_left2():
        middle[0].wait_recv()
        return rows(left2, 0, NB // 2)

    def take_left():
        middle[1].wait_recv()
        return jnp.concatenate([rows(left.at[h], 0, NB // 2) for h in range(2)], axis=0)

    def take_right():
        middle[2].wait_recv()
        store(0, OWN + NB, jnp.concatenate([rows(right.at[0], 0, NB // 2), rows(right.at[1], 0, 1)], axis=0))

    second = lax.rem(slab, 2) == 1

    @pl.when(jnp.logical_not(second))
    def _():
        take_right()
        advance(0, (OWN + 2, 9))
        advance(1, (OWN + 4, 5))
        advance(2, (OWN + 6, 1))
        store(0, OWN - NB - NB // 2, jnp.concatenate([take_left2(), take_left()], axis=0))
        for s in range(3):
            advance(s, (OWN - 10 + 2 * s, 12))

    @pl.when(second)
    def _():
        store(0, OWN - NB, take_left())
        advance(0, (OWN - 6, 12))
        advance(1, (OWN - 4, 8))
        advance(2, (OWN - 2, 4))
        store(0, OWN - NB - NB // 2, take_left2())
        take_right()
        for s in range(3):
            advance(s, (OWN - 10 + 2 * s, 4), (OWN + 6 - 2 * s, 5))

    for c in middle:
        c.wait_send()
    relay(1)

    for s in range(4, LAST + 1):
        reach = HALO * (LAST - s)
        lo, end = OWN - reach, OWN + reach + 1
        head = step(s - 1, (lo, end - lo))
        if s < LAST:
            store(s, lo, head)
        if s == 4:
            relay(2)

    row = lax.broadcasted_iota(jnp.int32, (8, BLOCK), 0)
    mine[...] = jnp.where(row < 3, head[0], 0.0)[0:4]
    for d in square:
        send(mine, plane.at[image], 7, in_plane(d)).start()

    later.wait()
    anchor[4] = rows(ahead, 0, 1)[0] * SCALE
    last.wait()
    store(0, OWN + NB + NB // 2 + 1, jnp.concatenate([rows(right.at[1], 1, NB // 2), rows(right2, 0, NB // 2)], axis=0))

    def rest_of_step(s):
        lo = OWN + HALO * (LAST - s) + 1
        y = step(s - 1, (lo, NB - 1))
        if s < LAST:
            store(s, lo, y)
        return y

    for s in range(1, LAST - 1):
        rest_of_step(s)
    others = plane.at[pl.ds(1, IMAGES - 1)]
    pltpu.make_async_copy(others, others, sems.at[1, 7]).wait()
    plane[image] = mine[...]

    every = plane[...]
    change = every[1:] - every[:-1]
    change = jnp.concatenate([jnp.zeros((1, 4, BLOCK), F32), change], axis=0)
    squares = jnp.sum(jnp.sum(change * change, axis=1), axis=1, keepdims=True)
    at_row = lax.broadcasted_iota(jnp.int32, (IMAGES, BLOCK), 0)
    at_lane = lax.broadcasted_iota(jnp.int32, (IMAGES, BLOCK), 1)
    part[...] = jnp.sum(jnp.where(at_row == at_lane, squares, 0.0), axis=0, keepdims=True)

    relay(3)
    for d in ring:
        send(part, parts.at[slab], 10, beside(d)).start()
    rest_of_step(LAST - 1)
    pack(raw, jnp.concatenate([head, rest_of_step(LAST)], axis=0))
    images = [send(raw, around.at[i], 8 + i, across(d)) for i, d in enumerate((1, -1))]
    for c in images:
        c.start()
    for c in images:
        c.wait()
    pltpu.make_async_copy(others, others, sems.at[0, 7]).wait()
    rest = parts.at[pl.ds(1, N_SPACE - 1)]
    pltpu.make_async_copy(rest, rest, sems.at[1, 10]).wait()
    parts[slab] = part[...]

    total_ref[...] = jnp.sum(parts[...], axis=0)
    images_ref[0] = around[0]
    images_ref[1] = raw[...]
    images_ref[2] = around[1]
    pltpu.make_async_copy(rest, rest, sems.at[0, 10]).wait()


def blend(images_ref, total_ref, whole_ref, out_ref, fraction_ref, out, fraction, sems):
    image = lax.axis_index("image")
    lane = lax.broadcasted_iota(jnp.int32, (1, BLOCK), 1)
    lengths = jnp.sqrt(total_ref[...] * (1.0 / SCALE**2) + EPSILON)
    lengths = jnp.where((lane > 0) & (lane < IMAGES), lengths, 0.0)

    def arc(k):
        return jnp.sum(jnp.where(lane <= k, lengths, 0.0), axis=1, keepdims=True)

    full = arc(IMAGES - 1)
    fraction[...] = jnp.broadcast_to(arc(image) / full, (1, BLOCK))
    lower = whole_ref[NEIGHBOURS : NEIGHBOURS + 1, :BLOCK]
    code = whole_ref[NEIGHBOURS + 1 : NEIGHBOURS + 2, :BLOCK]
    arc_lower = arc(lower)
    place = lower.astype(F32) + code.astype(F32) / CODE_SCALE
    weight = (place / (IMAGES - 1) * full - arc_lower) / (arc(lower + 1) - arc_lower)
    earlier = lower < image
    for c in range(3):
        here = images_ref[1, c]
        below = jnp.where(earlier, images_ref[0, c], here)
        above = jnp.where(earlier, here, images_ref[2, c])
        out[c] = ((1.0 - weight) * below + weight * above) * (1.0 / SCALE)
    stores = [pltpu.make_async_copy(s, d, sems.at[i]) for i, (s, d) in enumerate([(out, out_ref), (fraction, fraction_ref)])]
    for c in stores:
        c.start()
    for c in stores:
        c.wait()


def body(positions, neighbours, brackets, codes):
    vmem = pl.BlockSpec(memory_space=pltpu.VMEM)
    left, right = (
        lax.ppermute(positions, "space", [(i, (i + d) % N_SPACE) for i in range(N_SPACE)]) for d in (1, -1)
    )
    along = [jnp.broadcast_to(v[:, None], (1, BLOCKS)) for v in (brackets, codes)]
    whole = jnp.concatenate([neighbours.T] + along, axis=0)
    images, total = pl.pallas_call(
        kernel,
        out_shape=(jax.ShapeDtypeStruct((3, 3, NB, BLOCK), F32), jax.ShapeDtypeStruct((1, BLOCK), F32)),
        in_specs=[vmem] * 4,
        out_specs=(vmem, vmem),
        scratch_shapes=[
            pltpu.SMEM((NEIGHBOURS + 2, BLOCKS), jnp.int32),
            pltpu.SemaphoreType.DMA,
            pltpu.SemaphoreType.REGULAR((3,)),
            pltpu.VMEM((LAST, EXT, 8, BLOCK), F32),
            pltpu.VMEM((EXT // NB, 8, BLOCK), F32),
            pltpu.VMEM((LAST, EXT, BLOCK, 48), BF16),
            pltpu.VMEM((LAST, EXT, 48, BLOCK), BF16),
            pltpu.VMEM((LAST, EXT, 32, BLOCK), BF16),
            pltpu.VMEM((3, NB, BLOCK), F32),
            pltpu.VMEM((3, NB, BLOCK), F32),
            pltpu.VMEM((2, 3, NB // 2, BLOCK), F32),
            pltpu.VMEM((2, 3, NB // 2, BLOCK), F32),
            pltpu.VMEM((2, 2, 3, NB // 2, BLOCK), F32),
            pltpu.VMEM((2, 3, NB, BLOCK), F32),
            pltpu.VMEM((IMAGES, 4, BLOCK), F32),
            pltpu.VMEM((4, BLOCK), F32),
            pltpu.VMEM((1, BLOCK), F32),
            pltpu.VMEM((N_SPACE, 1, BLOCK), F32),
            pltpu.SemaphoreType.DMA((2, 11)),
        ],
        compiler_params=pltpu.CompilerParams(collective_id=0, has_side_effects=True, vmem_limit_bytes=48 << 20),
    )(*(x.reshape(3, NB, BLOCK) for x in (positions, left, right)), whole)
    hbm = pl.BlockSpec(memory_space=pl.ANY)
    out, fraction = pl.pallas_call(
        blend,
        out_shape=(jax.ShapeDtypeStruct((3, NB, BLOCK), F32), jax.ShapeDtypeStruct((1, BLOCK), F32)),
        in_specs=[vmem] * 3,
        out_specs=(hbm, hbm),
        scratch_shapes=[
            pltpu.VMEM((3, NB, BLOCK), F32),
            pltpu.VMEM((1, BLOCK), F32),
            pltpu.SemaphoreType.DMA((2,)),
        ],
        compiler_params=pltpu.CompilerParams(vmem_limit_bytes=16 << 20),
    )(images, total, whole)
    return out.reshape(1, 3, NB * BLOCK), fraction[0, :1]


def solution(mesh):
    placed = (P("image", None, "space"), P(), P("image"), P("image"))
    return jax.shard_map(
        body,
        mesh=mesh,
        in_specs=placed,
        out_specs=(P("image", None, "space"), P("image")),
        check_vma=False,
    )
```

```python
import functools
import math

import jax
import jax.numpy as jnp
from jax import lax
from jax.experimental import pallas as pl
from jax.experimental.pallas import tpu as pltpu
from jax.sharding import PartitionSpec as P

MESH = pl.DeviceIdType.MESH
F32, BF16 = jnp.float32, jnp.bfloat16

BLOCK = 128
HALO = 2
NB = 8
NEIGHBOURS = 3
IMAGES = 16
N_SPACE = 32
BLOCKS = NB * N_SPACE
TIME_STEP = 0.05
RESTRAINT = 1.0
COUPLING = 3.0
KERNEL_RATE = 0.125
EPSILON = 1e-06
CODE_SCALE = 65536.0

FIRST, LAST = 4, 6
OWN = 2 * NB
EXT = 5 * NB

SCALE = math.sqrt(KERNEL_RATE * math.log2(math.e))
PULL = TIME_STEP * COUPLING / (NEIGHBOURS * BLOCK)


def dot(a, b):
    return lax.dot_general(a, b, (((1,), (0,)), ((), ())), preferred_element_type=F32)


def split3(v):
    high = v.astype(BF16).astype(F32)
    rest = v - high
    middle = rest.astype(BF16).astype(F32)
    return high, middle, rest - middle


def operands(y):
    row = lax.broadcasted_iota(jnp.int32, y.shape, 1)
    y = jnp.where(row < 3, y, 0.0)
    square = jnp.sum(y * y, axis=1, keepdims=True)
    partner = jnp.where(row == 3, square, jnp.where(row == 4, 1.0, y))
    centre = jnp.where(row == 3, -1.0, jnp.where(row == 4, -square, y + y))
    ph, pm, plow = split3(partner)
    ch, cm, cl = split3(centre)
    a = jnp.concatenate([ph, ph, ph, pm, pm, plow], axis=1).astype(BF16)
    b = jnp.concatenate([ch, cm, cl, ch, cm, ch], axis=1).astype(BF16)
    x = jnp.concatenate([ph, pm, plow, jnp.zeros_like(y)], axis=1).astype(BF16)
    return a, b, x


def kernel(
    x_ref, left_ref, right_ref, table_in, images_ref, total_ref,
    table, local_sem, relay_sems, cur, anchor, aop, bop, xop, raw, ahead, halves, far, whole, around, plane, mine, part, parts, sems,
):
    image, slab = lax.axis_index("image"), lax.axis_index("space")

    def beside(d):
        return (image, lax.rem(slab + d + N_SPACE, N_SPACE))

    def across(d):
        return (lax.rem(image + d + IMAGES, IMAGES), slab)

    ring = sorted(range(1, N_SPACE), key=lambda d: -min(d, N_SPACE - d))
    square = [(dx, dy) for dx in range(4) for dy in range(4) if (dx, dy) != (0, 0)]
    square.sort(key=lambda d: -sum(min(v, 4 - v) for v in d))

    def in_plane(d):
        return (lax.rem(image // 4 + d[0], 4) * 4 + lax.rem(lax.rem(image, 4) + d[1], 4), slab)

    def greet(semaphore, peers):
        for peer in peers:
            pl.semaphore_signal(semaphore, inc=1, device_id=peer, device_id_type=MESH)

    barrier = pltpu.get_barrier_semaphore()
    near = [peer for d in (1, -1, 2, -2) for peer in (beside(d), across(d))]
    stages = [
        [peer for d in (2, -2) for peer in (beside(d), across(d))],
        [peer for d in (4, -4) for peer in (beside(d), across(d))],
        [beside(8), beside(-8)],
    ]

    def relay(j):
        if j > 0:
            pl.semaphore_wait(relay_sems.at[j - 1], len(stages[j - 1]))
        if j < len(stages):
            greet(relay_sems.at[j], stages[j])

    greet(barrier, near)
    load = pltpu.make_async_copy(table_in, table, local_sem)
    load.start()

    def store(version, lo, y):
        a, b, x = operands(y)
        n = y.shape[0]
        cur[version, lo : lo + n] = y
        bop[version, lo : lo + n] = b
        xop[version, lo : lo + n] = x
        for i in range(n):
            aop[version, lo + i] = a[i].T

    def rows(slab_ref, first, last):
        n = last - first
        coordinates = [slab_ref[c, first:last].reshape(n, 1, BLOCK) for c in range(3)]
        return jnp.concatenate(coordinates + [jnp.zeros((n, 5, BLOCK), F32)], axis=1)

    def send(source, target, slot, peer):
        return pltpu.make_async_remote_copy(
            src_ref=source, dst_ref=target, send_sem=sems.at[0, slot], recv_sem=sems.at[1, slot],
            device_id=peer, device_id_type=MESH,
        )

    def step(version, *runs):
        blocks = [e for lo, n in runs for e in range(lo, lo + n)]
        first = slab * NB + BLOCKS - OWN
        partners = [
            [e - HALO + table[k, lax.rem(first + e, BLOCKS)] for k in range(NEIGHBOURS)]
            for e in blocks
        ]
        weights = []
        for e, ps in zip(blocks, partners):
            exponent = dot(jnp.concatenate([aop[version, p] for p in ps], axis=0), bop[version, e])
            w = jnp.exp2(exponent)
            high = w.astype(BF16)
            weights.append(jnp.concatenate([high, (w - high.astype(F32)).astype(BF16)], axis=0))
        sums = []
        for ps, w in zip(partners, weights):
            x = jnp.concatenate([xop[version, p] for p in ps], axis=1)
            total = dot(jnp.concatenate([x, x], axis=1), w)
            sums.append(total[0:8] + total[8:16] + total[16:24])
        held = [cur[version, lo : lo + n] for lo, n in runs]
        y = jnp.concatenate(held, axis=0) if len(runs) > 1 else held[0]
        total = jnp.stack(sums, axis=0)
        y_new = y + PULL * (y * total[:, 4:5] - total)
        held = [
            y_new[i : i + 1] - (TIME_STEP * RESTRAINT) * (y[i : i + 1] - anchor[e // NB][None])
            if e % NB == 0
            else y_new[i : i + 1]
            for i, e in enumerate(blocks)
        ]
        return jnp.concatenate(held, axis=0) if len(held) > 1 else held[0]

    def pack(ref, y):
        for c in range(3):
            ref[c] = y[:, c]

    own, left, right = (rows(ref, 0, NB) * SCALE for ref in (x_ref, left_ref, right_ref))
    for i, y in enumerate((left, own, right)):
        anchor[1 + i] = y[0]
        store(0, OWN + (i - 1) * NB, y)
    load.wait()
    for t in range(FIRST):
        reach = HALO * (FIRST - 1 - t)
        y = step(0, (OWN - reach, NB + 2 * reach))
        if t < FIRST - 1:
            store(0, OWN - reach, y)
        if t == 1:
            pl.semaphore_wait(barrier, len(near))
            relay(0)
            later = send(x_ref, ahead, 0, beside(-2))
            later.start()

    for h in range(2):
        pack(halves.at[h], y[h * NB // 2 : (h + 1) * NB // 2])
    left2, left, right, right2 = far.at[0], whole.at[0], whole.at[1], far.at[1]
    middle = [
        send(halves.at[1], left2, 1, beside(2)),
        send(halves, left, 2, beside(1)),
        send(halves, right, 3, beside(-1)),
    ]
    for c in middle:
        c.start()
    last = send(halves.at[0], right2, 4, beside(-2))
    last.start()
    store(0, OWN, y)
    inner = (OWN + HALO, NB - 2 * HALO)
    store(1, inner[0], step(0, inner))
    for c in middle:
        c.wait()
    relay(1)
    left = jnp.concatenate([rows(left2, 0, NB // 2)] + [rows(left.at[h], 0, NB // 2) for h in range(2)], axis=0)
    store(0, OWN - NB - NB // 2, left)
    store(0, OWN + NB, jnp.concatenate([rows(right.at[0], 0, NB // 2), rows(right.at[1], 0, 1)], axis=0))

    for s in range(1, LAST + 1):
        reach = HALO * (LAST - s)
        lo, end = OWN - reach, OWN + reach + 1
        if s == 1:
            n = inner[0] - lo
            after = inner[0] + inner[1]
            head = step(0, (lo, n), (after, end - after))
            store(1, lo, head[:n])
            store(1, after, head[n:])
            continue
        head = step(s - 1, (lo, end - lo))
        if s < LAST:
            store(s, lo, head)
        if s == 4:
            relay(2)

    row = lax.broadcasted_iota(jnp.int32, (8, BLOCK), 0)
    mine[...] = jnp.where(row < 3, head[0], 0.0)[0:4]
    for d in square:
        send(mine, plane.at[image], 7, in_plane(d)).start()

    later.wait()
    anchor[4] = rows(ahead, 0, 1)[0] * SCALE
    last.wait()
    store(0, OWN + NB + NB // 2 + 1, jnp.concatenate([rows(right.at[1], 1, NB // 2), rows(right2, 0, NB // 2)], axis=0))

    def rest_of_step(s):
        lo = OWN + HALO * (LAST - s) + 1
        y = step(s - 1, (lo, NB - 1))
        if s < LAST:
            store(s, lo, y)
        return y

    for s in range(1, LAST - 1):
        rest_of_step(s)
    others = plane.at[pl.ds(1, IMAGES - 1)]
    pltpu.make_async_copy(others, others, sems.at[1, 7]).wait()
    plane[image] = mine[...]

    every = plane[...]
    change = every[1:] - every[:-1]
    change = jnp.concatenate([jnp.zeros((1, 4, BLOCK), F32), change], axis=0)
    squares = jnp.sum(jnp.sum(change * change, axis=1), axis=1, keepdims=True)
    at_row = lax.broadcasted_iota(jnp.int32, (IMAGES, BLOCK), 0)
    at_lane = lax.broadcasted_iota(jnp.int32, (IMAGES, BLOCK), 1)
    part[...] = jnp.sum(jnp.where(at_row == at_lane, squares, 0.0), axis=0, keepdims=True)

    relay(3)
    for d in ring:
        send(part, parts.at[slab], 10, beside(d)).start()
    rest_of_step(LAST - 1)
    pack(raw, jnp.concatenate([head, rest_of_step(LAST)], axis=0))
    images = [send(raw, around.at[i], 8 + i, across(d)) for i, d in enumerate((1, -1))]
    for c in images:
        c.start()
    for c in images:
        c.wait()
    pltpu.make_async_copy(others, others, sems.at[0, 7]).wait()
    rest = parts.at[pl.ds(1, N_SPACE - 1)]
    pltpu.make_async_copy(rest, rest, sems.at[1, 10]).wait()
    parts[slab] = part[...]

    total_ref[...] = jnp.sum(parts[...], axis=0)
    images_ref[0] = around[0]
    images_ref[1] = raw[...]
    images_ref[2] = around[1]
    pltpu.make_async_copy(rest, rest, sems.at[0, 10]).wait()


def blend(images_ref, total_ref, whole_ref, out_ref, fraction_ref, out, fraction, sems):
    image = lax.axis_index("image")
    lane = lax.broadcasted_iota(jnp.int32, (1, BLOCK), 1)
    lengths = jnp.sqrt(total_ref[...] * (1.0 / SCALE**2) + EPSILON)
    lengths = jnp.where((lane > 0) & (lane < IMAGES), lengths, 0.0)

    def arc(k):
        return jnp.sum(jnp.where(lane <= k, lengths, 0.0), axis=1, keepdims=True)

    full = arc(IMAGES - 1)
    fraction[...] = jnp.broadcast_to(arc(image) / full, (1, BLOCK))
    lower = whole_ref[NEIGHBOURS : NEIGHBOURS + 1, :BLOCK]
    code = whole_ref[NEIGHBOURS + 1 : NEIGHBOURS + 2, :BLOCK]
    arc_lower = arc(lower)
    place = lower.astype(F32) + code.astype(F32) / CODE_SCALE
    weight = (place / (IMAGES - 1) * full - arc_lower) / (arc(lower + 1) - arc_lower)
    earlier = lower < image
    for c in range(3):
        here = images_ref[1, c]
        below = jnp.where(earlier, images_ref[0, c], here)
        above = jnp.where(earlier, here, images_ref[2, c])
        out[c] = ((1.0 - weight) * below + weight * above) * (1.0 / SCALE)
    stores = [pltpu.make_async_copy(s, d, sems.at[i]) for i, (s, d) in enumerate([(out, out_ref), (fraction, fraction_ref)])]
    for c in stores:
        c.start()
    for c in stores:
        c.wait()


def body(positions, neighbours, brackets, codes):
    vmem = pl.BlockSpec(memory_space=pltpu.VMEM)
    left, right = (
        lax.ppermute(positions, "space", [(i, (i + d) % N_SPACE) for i in range(N_SPACE)]) for d in (1, -1)
    )
    along = [jnp.broadcast_to(v[:, None], (1, BLOCKS)) for v in (brackets, codes)]
    whole = jnp.concatenate([neighbours.T] + along, axis=0)
    images, total = pl.pallas_call(
        kernel,
        out_shape=(jax.ShapeDtypeStruct((3, 3, NB, BLOCK), F32), jax.ShapeDtypeStruct((1, BLOCK), F32)),
        in_specs=[vmem] * 4,
        out_specs=(vmem, vmem),
        scratch_shapes=[
            pltpu.SMEM((NEIGHBOURS + 2, BLOCKS), jnp.int32),
            pltpu.SemaphoreType.DMA,
            pltpu.SemaphoreType.REGULAR((3,)),
            pltpu.VMEM((LAST, EXT, 8, BLOCK), F32),
            pltpu.VMEM((EXT // NB, 8, BLOCK), F32),
            pltpu.VMEM((LAST, EXT, BLOCK, 48), BF16),
            pltpu.VMEM((LAST, EXT, 48, BLOCK), BF16),
            pltpu.VMEM((LAST, EXT, 32, BLOCK), BF16),
            pltpu.VMEM((3, NB, BLOCK), F32),
            pltpu.VMEM((3, NB, BLOCK), F32),
            pltpu.VMEM((2, 3, NB // 2, BLOCK), F32),
            pltpu.VMEM((2, 3, NB // 2, BLOCK), F32),
            pltpu.VMEM((2, 2, 3, NB // 2, BLOCK), F32),
            pltpu.VMEM((2, 3, NB, BLOCK), F32),
            pltpu.VMEM((IMAGES, 4, BLOCK), F32),
            pltpu.VMEM((4, BLOCK), F32),
            pltpu.VMEM((1, BLOCK), F32),
            pltpu.VMEM((N_SPACE, 1, BLOCK), F32),
            pltpu.SemaphoreType.DMA((2, 11)),
        ],
        compiler_params=pltpu.CompilerParams(collective_id=0, has_side_effects=True, vmem_limit_bytes=48 << 20),
    )(*(x.reshape(3, NB, BLOCK) for x in (positions, left, right)), whole)
    hbm = pl.BlockSpec(memory_space=pl.ANY)
    out, fraction = pl.pallas_call(
        blend,
        out_shape=(jax.ShapeDtypeStruct((3, NB, BLOCK), F32), jax.ShapeDtypeStruct((1, BLOCK), F32)),
        in_specs=[vmem] * 3,
        out_specs=(hbm, hbm),
        scratch_shapes=[
            pltpu.VMEM((3, NB, BLOCK), F32),
            pltpu.VMEM((1, BLOCK), F32),
            pltpu.SemaphoreType.DMA((2,)),
        ],
        compiler_params=pltpu.CompilerParams(vmem_limit_bytes=16 << 20),
    )(images, total, whole)
    return out.reshape(1, 3, NB * BLOCK), fraction[0, :1]


def solution(mesh):
    placed = (P("image", None, "space"), P(), P("image"), P("image"))
    return jax.shard_map(
        body,
        mesh=mesh,
        in_specs=placed,
        out_specs=(P("image", None, "space"), P("image")),
        check_vma=False,
    )
```

```python
import functools
import math

import jax
import jax.numpy as jnp
from jax import lax
from jax.experimental import pallas as pl
from jax.experimental.pallas import tpu as pltpu
from jax.sharding import PartitionSpec as P

MESH = pl.DeviceIdType.MESH
F32, BF16 = jnp.float32, jnp.bfloat16

BLOCK = 128
HALO = 2
NB = 8
NEIGHBOURS = 3
IMAGES = 16
N_SPACE = 32
BLOCKS = NB * N_SPACE
TIME_STEP = 0.05
RESTRAINT = 1.0
COUPLING = 3.0
KERNEL_RATE = 0.125
EPSILON = 1e-06
CODE_SCALE = 65536.0

FIRST, LAST = 4, 6
OWN = 2 * NB
EXT = 5 * NB

SCALE = math.sqrt(KERNEL_RATE * math.log2(math.e))
PULL = TIME_STEP * COUPLING / (NEIGHBOURS * BLOCK)


def dot(a, b):
    return lax.dot_general(a, b, (((1,), (0,)), ((), ())), preferred_element_type=F32)


def split3(v):
    high = v.astype(BF16).astype(F32)
    rest = v - high
    middle = rest.astype(BF16).astype(F32)
    return high, middle, rest - middle


def operands(y):
    row = lax.broadcasted_iota(jnp.int32, y.shape, 1)
    y = jnp.where(row < 3, y, 0.0)
    square = jnp.sum(y * y, axis=1, keepdims=True)
    partner = jnp.where(row == 3, square, jnp.where(row == 4, 1.0, y))
    centre = jnp.where(row == 3, -1.0, jnp.where(row == 4, -square, y + y))
    ph, pm, plow = split3(partner)
    ch, cm, cl = split3(centre)
    a = jnp.concatenate([ph, ph, ph, pm, pm, plow], axis=1).astype(BF16)
    b = jnp.concatenate([ch, cm, cl, ch, cm, ch], axis=1).astype(BF16)
    x = jnp.concatenate([ph, pm, plow, jnp.zeros_like(y)], axis=1).astype(BF16)
    return a, b, x


def kernel(
    x_ref, right_ref, left_ref, table_in, images_ref, total_ref,
    table, local_sem, relay_sems, cur, anchor, aop, bop, xop, raw, ahead, halves, far, whole, around, plane, mine, part, parts, sems,
):
    image, slab = lax.axis_index("image"), lax.axis_index("space")

    def beside(d):
        return (image, lax.rem(slab + d + N_SPACE, N_SPACE))

    def across(d):
        return (lax.rem(image + d + IMAGES, IMAGES), slab)

    ring = sorted(range(1, N_SPACE), key=lambda d: -min(d, N_SPACE - d))
    square = [(dx, dy) for dx in range(4) for dy in range(4) if (dx, dy) != (0, 0)]
    square.sort(key=lambda d: -sum(min(v, 4 - v) for v in d))

    def in_plane(d):
        return (lax.rem(image // 4 + d[0], 4) * 4 + lax.rem(lax.rem(image, 4) + d[1], 4), slab)

    def greet(semaphore, peers):
        for peer in peers:
            pl.semaphore_signal(semaphore, inc=1, device_id=peer, device_id_type=MESH)

    barrier = pltpu.get_barrier_semaphore()
    near = [peer for d in (1, -1, 2, -2) for peer in (beside(d), across(d))]
    stages = [
        [peer for d in (2, -2) for peer in (beside(d), across(d))],
        [peer for d in (4, -4) for peer in (beside(d), across(d))],
        [beside(8), beside(-8)],
    ]

    def relay(j):
        if j > 0:
            pl.semaphore_wait(relay_sems.at[j - 1], len(stages[j - 1]))
        if j < len(stages):
            greet(relay_sems.at[j], stages[j])

    greet(barrier, near)
    load = pltpu.make_async_copy(table_in, table, local_sem)
    load.start()

    def store(version, lo, y):
        a, b, x = operands(y)
        n = y.shape[0]
        cur[version, lo : lo + n] = y
        bop[version, lo : lo + n] = b
        xop[version, lo : lo + n] = x
        for i in range(n):
            aop[version, lo + i] = a[i].T

    def rows(slab_ref, first, last):
        n = last - first
        coordinates = [slab_ref[c, first:last].reshape(n, 1, BLOCK) for c in range(3)]
        return jnp.concatenate(coordinates + [jnp.zeros((n, 5, BLOCK), F32)], axis=1)

    def send(source, target, slot, peer):
        return pltpu.make_async_remote_copy(
            src_ref=source, dst_ref=target, send_sem=sems.at[0, slot], recv_sem=sems.at[1, slot],
            device_id=peer, device_id_type=MESH,
        )

    def step(version, *runs):
        blocks = [e for lo, n in runs for e in range(lo, lo + n)]
        first = slab * NB + BLOCKS - OWN
        partners = [
            [e - HALO + table[k, lax.rem(first + e, BLOCKS)] for k in range(NEIGHBOURS)]
            for e in blocks
        ]
        weights = []
        for e, ps in zip(blocks, partners):
            exponent = dot(jnp.concatenate([aop[version, p] for p in ps], axis=0), bop[version, e])
            w = jnp.exp2(exponent)
            high = w.astype(BF16)
            weights.append(jnp.concatenate([high, (w - high.astype(F32)).astype(BF16)], axis=0))
        sums = []
        for ps, w in zip(partners, weights):
            x = jnp.concatenate([xop[version, p] for p in ps], axis=1)
            total = dot(jnp.concatenate([x, x], axis=1), w)
            sums.append(total[0:8] + total[8:16] + total[16:24])
        held = [cur[version, lo : lo + n] for lo, n in runs]
        y = jnp.concatenate(held, axis=0) if len(runs) > 1 else held[0]
        total = jnp.stack(sums, axis=0)
        y_new = y + PULL * (y * total[:, 4:5] - total)
        held = [
            y_new[i : i + 1] - (TIME_STEP * RESTRAINT) * (y[i : i + 1] - anchor[e // NB][None])
            if e % NB == 0
            else y_new[i : i + 1]
            for i, e in enumerate(blocks)
        ]
        return jnp.concatenate(held, axis=0) if len(held) > 1 else held[0]

    def pack(ref, y):
        for c in range(3):
            ref[c] = y[:, c]

    own, left, right = (rows(ref, 0, NB) * SCALE for ref in (x_ref, left_ref, right_ref))
    for i, y in enumerate((left, own, right)):
        anchor[1 + i] = y[0]
        store(0, OWN + (i - 1) * NB, y)
    load.wait()
    for t in range(FIRST):
        reach = HALO * (FIRST - 1 - t)
        y = step(0, (OWN - reach, NB + 2 * reach))
        if t < FIRST - 1:
            store(0, OWN - reach, y)
        if t == 1:
            pl.semaphore_wait(barrier, len(near))
            relay(0)
            later = send(x_ref, ahead, 0, beside(-2))
            later.start()

    for h in range(2):
        pack(halves.at[h], y[h * NB // 2 : (h + 1) * NB // 2])
    left2, left, right, right2 = far.at[0], whole.at[0], whole.at[1], far.at[1]
    middle = [
        send(halves.at[1], left2, 1, beside(2)),
        send(halves, left, 2, beside(1)),
        send(halves, right, 3, beside(-1)),
    ]
    for c in middle:
        c.start()
    last = send(halves.at[0], right2, 4, beside(-2))
    last.start()
    store(0, OWN, y)
    inner = (OWN + HALO, NB - 2 * HALO)
    store(1, inner[0], step(0, inner))
    for c in middle:
        c.wait()
    relay(1)
    left = jnp.concatenate([rows(left2, 0, NB // 2)] + [rows(left.at[h], 0, NB // 2) for h in range(2)], axis=0)
    store(0, OWN - NB - NB // 2, left)
    store(0, OWN + NB, jnp.concatenate([rows(right.at[0], 0, NB // 2), rows(right.at[1], 0, 1)], axis=0))

    for s in range(1, LAST + 1):
        reach = HALO * (LAST - s)
        lo, end = OWN - reach, OWN + reach + 1
        if s == 1:
            n = inner[0] - lo
            after = inner[0] + inner[1]
            head = step(0, (lo, n), (after, end - after))
            store(1, lo, head[:n])
            store(1, after, head[n:])
            continue
        head = step(s - 1, (lo, end - lo))
        if s < LAST:
            store(s, lo, head)
        if s == 4:
            relay(2)

    row = lax.broadcasted_iota(jnp.int32, (8, BLOCK), 0)
    mine[...] = jnp.where(row < 3, head[0], 0.0)[0:4]
    for d in square:
        send(mine, plane.at[image], 7, in_plane(d)).start()

    later.wait()
    anchor[4] = rows(ahead, 0, 1)[0] * SCALE
    last.wait()
    store(0, OWN + NB + NB // 2 + 1, jnp.concatenate([rows(right.at[1], 1, NB // 2), rows(right2, 0, NB // 2)], axis=0))

    def rest_of_step(s):
        lo = OWN + HALO * (LAST - s) + 1
        y = step(s - 1, (lo, NB - 1))
        if s < LAST:
            store(s, lo, y)
        return y

    for s in range(1, LAST - 1):
        rest_of_step(s)
    others = plane.at[pl.ds(1, IMAGES - 1)]
    pltpu.make_async_copy(others, others, sems.at[1, 7]).wait()
    plane[image] = mine[...]

    every = plane[...]
    change = every[1:] - every[:-1]
    change = jnp.concatenate([jnp.zeros((1, 4, BLOCK), F32), change], axis=0)
    squares = jnp.sum(jnp.sum(change * change, axis=1), axis=1, keepdims=True)
    at_row = lax.broadcasted_iota(jnp.int32, (IMAGES, BLOCK), 0)
    at_lane = lax.broadcasted_iota(jnp.int32, (IMAGES, BLOCK), 1)
    part[...] = jnp.sum(jnp.where(at_row == at_lane, squares, 0.0), axis=0, keepdims=True)

    relay(3)
    for d in ring:
        send(part, parts.at[slab], 10, beside(d)).start()
    rest_of_step(LAST - 1)
    pack(raw, jnp.concatenate([head, rest_of_step(LAST)], axis=0))
    images = [send(raw, around.at[i], 8 + i, across(d)) for i, d in enumerate((1, -1))]
    for c in images:
        c.start()
    for c in images:
        c.wait()
    pltpu.make_async_copy(others, others, sems.at[0, 7]).wait()
    rest = parts.at[pl.ds(1, N_SPACE - 1)]
    pltpu.make_async_copy(rest, rest, sems.at[1, 10]).wait()
    parts[slab] = part[...]

    total_ref[...] = jnp.sum(parts[...], axis=0)
    images_ref[0] = around[0]
    images_ref[1] = raw[...]
    images_ref[2] = around[1]
    pltpu.make_async_copy(rest, rest, sems.at[0, 10]).wait()


def blend(images_ref, total_ref, whole_ref, out_ref, fraction_ref, out, fraction, sems):
    image = lax.axis_index("image")
    lane = lax.broadcasted_iota(jnp.int32, (1, BLOCK), 1)
    lengths = jnp.sqrt(total_ref[...] * (1.0 / SCALE**2) + EPSILON)
    lengths = jnp.where((lane > 0) & (lane < IMAGES), lengths, 0.0)

    def arc(k):
        return jnp.sum(jnp.where(lane <= k, lengths, 0.0), axis=1, keepdims=True)

    full = arc(IMAGES - 1)
    fraction[...] = jnp.broadcast_to(arc(image) / full, (1, BLOCK))
    lower = whole_ref[NEIGHBOURS : NEIGHBOURS + 1, :BLOCK]
    code = whole_ref[NEIGHBOURS + 1 : NEIGHBOURS + 2, :BLOCK]
    arc_lower = arc(lower)
    place = lower.astype(F32) + code.astype(F32) / CODE_SCALE
    weight = (place / (IMAGES - 1) * full - arc_lower) / (arc(lower + 1) - arc_lower)
    earlier = lower < image
    for c in range(3):
        here = images_ref[1, c]
        below = jnp.where(earlier, images_ref[0, c], here)
        above = jnp.where(earlier, here, images_ref[2, c])
        out[c] = ((1.0 - weight) * below + weight * above) * (1.0 / SCALE)
    stores = [pltpu.make_async_copy(s, d, sems.at[i]) for i, (s, d) in enumerate([(out, out_ref), (fraction, fraction_ref)])]
    for c in stores:
        c.start()
    for c in stores:
        c.wait()


def body(positions, neighbours, brackets, codes):
    vmem = pl.BlockSpec(memory_space=pltpu.VMEM)
    left, right = (
        lax.ppermute(positions, "space", [(i, (i + d) % N_SPACE) for i in range(N_SPACE)]) for d in (1, -1)
    )
    along = [jnp.broadcast_to(v[:, None], (1, BLOCKS)) for v in (brackets, codes)]
    whole = jnp.concatenate([neighbours.T] + along, axis=0)
    images, total = pl.pallas_call(
        kernel,
        out_shape=(jax.ShapeDtypeStruct((3, 3, NB, BLOCK), F32), jax.ShapeDtypeStruct((1, BLOCK), F32)),
        in_specs=[vmem] * 4,
        out_specs=(vmem, vmem),
        scratch_shapes=[
            pltpu.SMEM((NEIGHBOURS + 2, BLOCKS), jnp.int32),
            pltpu.SemaphoreType.DMA,
            pltpu.SemaphoreType.REGULAR((3,)),
            pltpu.VMEM((LAST, EXT, 8, BLOCK), F32),
            pltpu.VMEM((EXT // NB, 8, BLOCK), F32),
            pltpu.VMEM((LAST, EXT, BLOCK, 48), BF16),
            pltpu.VMEM((LAST, EXT, 48, BLOCK), BF16),
            pltpu.VMEM((LAST, EXT, 32, BLOCK), BF16),
            pltpu.VMEM((3, NB, BLOCK), F32),
            pltpu.VMEM((3, NB, BLOCK), F32),
            pltpu.VMEM((2, 3, NB // 2, BLOCK), F32),
            pltpu.VMEM((2, 3, NB // 2, BLOCK), F32),
            pltpu.VMEM((2, 2, 3, NB // 2, BLOCK), F32),
            pltpu.VMEM((2, 3, NB, BLOCK), F32),
            pltpu.VMEM((IMAGES, 4, BLOCK), F32),
            pltpu.VMEM((4, BLOCK), F32),
            pltpu.VMEM((1, BLOCK), F32),
            pltpu.VMEM((N_SPACE, 1, BLOCK), F32),
            pltpu.SemaphoreType.DMA((2, 11)),
        ],
        compiler_params=pltpu.CompilerParams(collective_id=0, has_side_effects=True, vmem_limit_bytes=48 << 20),
    )(*(x.reshape(3, NB, BLOCK) for x in (positions, right, left)), whole)
    hbm = pl.BlockSpec(memory_space=pl.ANY)
    out, fraction = pl.pallas_call(
        blend,
        out_shape=(jax.ShapeDtypeStruct((3, NB, BLOCK), F32), jax.ShapeDtypeStruct((1, BLOCK), F32)),
        in_specs=[vmem] * 3,
        out_specs=(hbm, hbm),
        scratch_shapes=[
            pltpu.VMEM((3, NB, BLOCK), F32),
            pltpu.VMEM((1, BLOCK), F32),
            pltpu.SemaphoreType.DMA((2,)),
        ],
        compiler_params=pltpu.CompilerParams(vmem_limit_bytes=16 << 20),
    )(images, total, whole)
    return out.reshape(1, 3, NB * BLOCK), fraction[0, :1]


def solution(mesh):
    placed = (P("image", None, "space"), P(), P("image"), P("image"))
    return jax.shard_map(
        body,
        mesh=mesh,
        in_specs=placed,
        out_specs=(P("image", None, "space"), P("image")),
        check_vma=False,
    )
```
